512 devices in a mesh: pipe: 32 (over y, x), expert: 16 (over z, core).
Axes of the slice: x: 4, y: 8, z: 8, core: 2. Of those that a mesh axis runs over, the one named last changes fastest.
Arguments:
- acts: bfloat16 [2048, 3072], P('expert'), may hold values from -6 to 6
- cotangent: bfloat16 [2048, 3072], P('expert'), may hold values from -6 to 6
- norm_gain: float32 [3072], replicated, may hold values from 0.5 to 1.5
- router: bfloat16 [3072, 16], replicated, may hold values from -0.109375 to 0.109375
- expert_ids: int32 [2048, 4], P('expert'), may hold values from 0 to 15, all different within a row; in each aligned block of 128 rows (0 to 127, 128 to 255, ...) at most 34 rows name the same one
- w_gate: bfloat16 [16, 3072, 5376], P('expert', None, 'pipe'), may hold values from -0.109375 to 0.109375
- w_up: bfloat16 [16, 3072, 5376], P('expert', None, 'pipe'), may hold values from -0.109375 to 0.109375
- w_down: bfloat16 [16, 5376, 3072], P('expert', 'pipe'), may hold values from -0.078125 to 0.078125
Outputs:
- grad_in: float32 [32, 64, 3072], P('pipe', 'expert')
The draws below stay inside these ranges and needn't reach their ends.
Inputs may be any that keep to these rules, and one draw needn't show every extreme that they name: `expert_ids`: each row names 4 different experts. In each aligned block of 128 rows (the tokens of one index of the expert axis) no expert is named by more than 34 rows, a bound that some block reaches.
All inputs are finite; a program needn't handle non-finite values.
Results may differ from the reference program's by a relative error of at most 0.007.
Values may be sent and summed in bfloat16 or wider, within the bound.
No kernel may reach another device: no remote copies, remote signals or barrier semaphores. Data moves between devices by JAX's collectives and lax.ppermute only.
A program may use at most 128 MiB of HBM per device.

```python
import math
import jax
import jax.numpy as jnp
import numpy as np
from jax import lax

D = 3072
FF = 5376
TOP = 4
TOK_DEV = 128
EXPERTS = 16
TOKENS = 2048
CAP = 34
N_PIPE = 32
N_EXPERT = 16


def block_levels(rng, dims, pieces, smallest, largest):
    factor_of, own = 1.0, jax.random.fold_in(rng, 6)
    for dim, shards_of in pieces:
        steps = jnp.exp(jax.random.uniform(jax.random.fold_in(own, dim), (shards_of,), jnp.float32, smallest / len(pieces), largest / len(pieces)))
        factor_of = factor_of * jnp.repeat(steps, dims[dim] // shards_of).reshape([-1 if axis == dim else 1 for axis in range(len(dims))])
    return factor_of


def assign_block(own_key, own, number, rows, count, top, most, lean):
    ranking = jax.random.permutation(own_key, count)
    heavy_load, ordinary = shares(count, rows * top, most, lean, True), shares(count, rows * top, most, lean, False)
    places = jnp.arange(count)

    def named(lengths, turn):
        used = int((lengths > 0).sum())
        fixed = max(1, used // 4)
        shifted = fixed + (places - fixed + turn * (used - fixed)) % max(1, count - fixed)
        return jnp.zeros((count,), jnp.int32).at[ranking[jnp.where(places < fixed, places, shifted)]].set(jnp.asarray(lengths, jnp.int32))

    lengths = jnp.where(number % 4 == 0, named(heavy_load, number // 4), named(ordinary, number - number // 4 - 1))
    mixed = jax.random.permutation(jax.random.fold_in(own, 3), count)
    source_of, sink = mixed[0:count // 2 * 2:2], mixed[1:count // 2 * 2:2]
    room = jnp.minimum(lengths[source_of] - 1, most - lengths[sink]) // 2
    room = jnp.where((source_of == ranking[0]) | (sink == ranking[0]) | (lengths[sink] == 0), 0, jnp.maximum(room, 0))
    shifted = jax.random.randint(jax.random.fold_in(own, 4), (count // 2,), 0, 1 << 20) % (room + 1)
    lengths = lengths.at[source_of].add(-shifted).at[sink].add(shifted)
    labels = jnp.searchsorted(jnp.cumsum(lengths), jnp.arange(rows * top), side="right").astype(jnp.int32)
    table = labels.reshape(top, rows).T
    table = table[jax.random.permutation(jax.random.fold_in(own, 1), rows)]
    turn = jax.random.randint(jax.random.fold_in(own, 2), (rows, 1), 0, top)
    return jnp.take_along_axis(table, (jnp.arange(top)[None, :] + turn) % top, axis=1)


def shares(amount, total, reach, slope, full):
    loads = [(1 << 20) // math.isqrt(grade ** slope) + 1 for grade in range(1, amount + 1)]
    largest = reach if full else min(reach, max(-(-total // amount), total * loads[0] // sum(loads)))
    least = 1 if total - largest >= amount - 1 else 0
    given, spare = [largest] + [least] * (amount - 1), total - largest - least * (amount - 1)
    while spare > 0:
        free = [i for i in range(1, amount) if given[i] < largest] or [i for i in range(1, amount) if given[i] < reach]
        mass, remaining = sum([loads[i] for i in free]), spare
        for i in free:
            extra = min(reach - given[i], max(1, remaining * loads[i] // mass), spare)
            given[i] = given[i] + extra
            spare = spare - extra
    return np.array(given)


def bell_draw(key, extent, spread, limit, shards=(), kind=jnp.bfloat16):
    drawn = spread * jax.random.normal(key, extent, jnp.float32)
    if shards:
        drawn = drawn * block_levels(key, extent, shards, -0.22, 0.18)
    return jnp.clip(drawn, -limit, limit).astype(kind)


def setup_inputs(seed: int = 0) -> dict:
    streams_of = jax.random.split(jax.random.key(seed), 9)
    acts = bell_draw(streams_of[0], (TOKENS, D), 1.0, 6.0, ((0, 16),))
    cotangent = bell_draw(streams_of[1], (TOKENS, D), 1.0, 6.0, ((0, 16),))
    norm_gain = jnp.clip(1.0 + 0.1 * jax.random.normal(streams_of[2], (D,), jnp.float32), 0.5, 1.5)
    router = bell_draw(streams_of[3], (D, EXPERTS), D ** -0.5, 0.109375)
    expert_ids_keys = jax.random.split(jax.random.fold_in(streams_of[4], 1), TOKENS // TOK_DEV)
    expert_ids_turns = jax.random.permutation(jax.random.fold_in(streams_of[4], 3), TOKENS // TOK_DEV)
    expert_ids = jax.vmap(lambda own, number: assign_block(jax.random.fold_in(streams_of[4], 2), own, number, TOK_DEV, EXPERTS, TOP, CAP, 1))(expert_ids_keys, expert_ids_turns).reshape((TOKENS, TOP))
    w_gate = bell_draw(streams_of[5], (EXPERTS, D, FF), D ** -0.5, 0.109375, ((0, 16), (2, 32)))
    w_up = bell_draw(streams_of[6], (EXPERTS, D, FF), D ** -0.5, 0.109375, ((0, 16), (2, 32)))
    w_down = bell_draw(streams_of[7], (EXPERTS, FF, D), FF ** -0.5, 0.078125, ((0, 16), (1, 32)))
    return {"acts": acts, "cotangent": cotangent, "norm_gain": norm_gain, "router": router, "expert_ids": expert_ids, "w_gate": w_gate, "w_up": w_up, "w_down": w_down}


eps = 1e-05

def normed(rows, gain):
    wide = rows.astype(jnp.float32)
    return wide * lax.rsqrt(lax.optimization_barrier(jnp.mean(wide * wide, axis=-1, keepdims=True)) + eps) * gain

def slot_table(ids, cap, experts):
    flat = ids.reshape(-1).astype(jnp.int32)
    pairs = flat.shape[0]
    onehot = (flat[:, None] == jnp.arange(experts, dtype=jnp.int32)[None, :]).astype(jnp.int32)
    before = jnp.cumsum(onehot, axis=0) - onehot
    place = lax.optimization_barrier(jnp.sum(onehot * before, axis=1)).astype(jnp.int32)
    slot = (flat * cap + place).astype(jnp.int32)
    table = jnp.full((experts * cap,), pairs, jnp.int32).at[slot].set(jnp.arange(pairs, dtype=jnp.int32))
    return (slot, table)

def token_front(x, gain, router_w, ids, cap):
    tokens, top = ids.shape
    experts = router_w.shape[1]
    h = normed(x, gain).astype(jnp.bfloat16)
    logits = jnp.dot(h, router_w, preferred_element_type=jnp.float32)
    select = (ids[:, :, None] == jnp.arange(experts, dtype=jnp.int32)[None, None, :]).astype(jnp.float32)
    picked = jnp.einsum('tke,te->tk', select, logits)
    sig = jax.nn.sigmoid(picked)
    total = lax.optimization_barrier(jnp.sum(sig, axis=1, keepdims=True))
    weight = sig / total
    slot, table = slot_table(ids, cap, experts)
    pairs = tokens * top
    valid = table < pairs
    source = jnp.minimum(table, pairs - 1)
    owner = source // top
    return (h, sig, total, weight, select, slot, valid, owner, source)

def pack_rows(rows, valid, owner, experts, cap):
    width = rows.shape[1]
    return jnp.where(valid[:, None], rows[owner], jnp.zeros((), rows.dtype)).reshape(experts, cap, width)

def weighted_rows(weight, grads, valid, owner, source, experts, cap):
    gate_rows = weight.reshape(-1)[source].astype(jnp.bfloat16).astype(jnp.float32)
    scaled = (gate_rows[:, None] * grads[owner].astype(jnp.float32)).astype(jnp.bfloat16)
    return jnp.where(valid[:, None], scaled, jnp.zeros((), jnp.bfloat16)).reshape(experts, cap, grads.shape[1])

def expert_rows(rows, dy_rows, w_both, wd):
    contract = (((1,), (1,)), ((), ()))
    hidden = wd.shape[0]
    both = jnp.dot(rows, w_both, preferred_element_type=jnp.float32)
    a_part = both[:, :hidden]
    b_part = both[:, hidden:]
    sg = jax.nn.sigmoid(a_part)
    sa = a_part * sg
    act = (sa * b_part).astype(jnp.bfloat16)
    y_rows = jnp.dot(act, wd, preferred_element_type=jnp.float32)
    dact = lax.dot_general(dy_rows, wd, contract, preferred_element_type=jnp.float32)
    da_rows = (dact * b_part * sg * (1.0 + a_part * (1.0 - sg))).astype(jnp.bfloat16)
    db_rows = (dact * sa).astype(jnp.bfloat16)
    dboth = jnp.concatenate([da_rows, db_rows], axis=1)
    dh_rows = lax.dot_general(dboth, w_both, contract, preferred_element_type=jnp.float32)
    return (dh_rows, y_rows)

def sum_pairs(back_dh, slot, tokens, top):
    width = back_dh.shape[-1]
    return lax.optimization_barrier(jnp.sum(back_dh.reshape(-1, width)[slot].reshape(tokens, top, width), axis=1))

def token_back(x, g, gain, router_w, dh_tok, dscore, sig, total, weight, select):
    dsig = (dscore - lax.optimization_barrier(jnp.sum(weight * dscore, axis=1, keepdims=True))) / total
    dpick = dsig * sig * (1.0 - sig)
    dlogits = jnp.einsum('tk,tke->te', dpick, select)
    dh_total = dh_tok + lax.dot_general(dlogits, router_w.astype(jnp.float32), (((1,), (1,)), ((), ())))
    wide = x.astype(jnp.float32)
    recip = lax.rsqrt(lax.optimization_barrier(jnp.mean(wide * wide, axis=-1, keepdims=True)) + eps)
    scaled = dh_total * gain
    pulled = recip * scaled - wide * (recip * recip * recip) * lax.optimization_barrier(jnp.mean(wide * scaled, axis=-1, keepdims=True))
    return g.astype(jnp.float32) + pulled

def reference(acts, cotangent, norm_gain, router, expert_ids, w_gate, w_up, w_down):
    blocks = N_EXPERT
    xb = acts.reshape(blocks, TOK_DEV, D)
    gb = cotangent.reshape(blocks, TOK_DEV, D)
    ib = expert_ids.reshape(blocks, TOK_DEV, TOP)

    def front(xx, gg, ii):
        h, sig, total, weight, select, slot, valid, owner, source = token_front(xx, norm_gain, router, ii, CAP)
        send_h = pack_rows(h, valid, owner, EXPERTS, CAP)
        send_dy = weighted_rows(weight, gg, valid, owner, source, EXPERTS, CAP)
        return (send_h, send_dy, sig, total, weight, select, slot)
    send_h, send_dy, sig, total, weight, select, slot = jax.vmap(front)(xb, gb, ib)

    def one_expert(parts):
        hh, dd, wge, wue, wde = parts
        w_both = jnp.concatenate([wge, wue], axis=1)
        return expert_rows(hh.reshape(-1, D), dd.reshape(-1, D), w_both, wde)
    dh_all, y_all = lax.map(one_expert, (jnp.swapaxes(send_h, 0, 1), jnp.swapaxes(send_dy, 0, 1), w_gate, w_up, w_down))
    back_dh = jnp.swapaxes(dh_all.reshape(EXPERTS, blocks, CAP, D), 0, 1)
    back_y = jnp.swapaxes(y_all.reshape(EXPERTS, blocks, CAP, D), 0, 1)

    def back(xx, gg, bd, by, sg, tt, wt, sl, st):
        dh_tok = sum_pairs(bd, st, TOK_DEV, TOP)
        y_pairs = by.reshape(-1, D)[st].reshape(TOK_DEV, TOP, D)
        dscore = lax.optimization_barrier(jnp.sum(y_pairs * gg.astype(jnp.float32)[:, None, :], axis=-1))
        return token_back(xx, gg, norm_gain, router, dh_tok, dscore, sg, tt, wt, sl)
    dx = jax.vmap(back)(xb, gb, back_dh, back_y, sig, total, weight, select, slot)
    split = jnp.swapaxes(dx.reshape(blocks, N_PIPE, TOK_DEV // N_PIPE, D), 0, 1)
    return split.reshape(N_PIPE, TOKENS // N_PIPE, D)
```

```python
import jax
import jax.numpy as jnp
import numpy as np
from jax import lax
from jax.sharding import Mesh, PartitionSpec as P

eps = 1e-05
X = 4
CORES = 2
bf16 = jnp.bfloat16
f32 = jnp.float32


def token_weights(acts, gain, router, ids):
    wide = acts.astype(f32)
    recip = lax.rsqrt(jnp.mean(wide * wide, axis=-1, keepdims=True) + eps)
    h = (wide * recip * gain).astype(bf16)
    logits = jnp.dot(h, router, preferred_element_type=f32)
    experts = router.shape[1]
    select = (ids[:, :, None] == jnp.arange(experts, dtype=jnp.int32)[None, None, :]).astype(f32)
    picked = jnp.sum(select * logits[:, None, :], axis=-1)
    sig = jax.nn.sigmoid(picked)
    total = jnp.sum(sig, axis=1, keepdims=True)
    return h, sig, total, sig / total, select


def slots(ids, names, cap):
    tokens = ids.shape[0]
    member = jnp.any(ids[:, :, None] == names[None, None, :], axis=1)
    below = (jnp.arange(tokens)[:, None] > jnp.arange(tokens)[None, :]).astype(bf16)
    place = jnp.dot(below, member.astype(bf16), preferred_element_type=f32).astype(jnp.int32)
    place = jnp.where(member, place, cap)
    return place.T[:, None, :] == jnp.arange(cap, dtype=jnp.int32)[None, :, None]


def expert_rows(h, g, gate_rows, units):
    contract = (((1,), (1,)), ((), ()))
    dh = 0.0
    score = 0.0
    for wg, wu, wd in units:
        a = jnp.dot(h, wg, preferred_element_type=f32)
        b = jnp.dot(h, wu, preferred_element_type=f32)
        pulled = lax.dot_general(g, wd, contract, preferred_element_type=f32)
        sg = jax.nn.sigmoid(a)
        sa = a * sg
        act = (sa * b).astype(bf16).astype(f32)
        score = score + jnp.sum(act * pulled, axis=-1)
        dact = pulled * gate_rows
        da = (dact * b * sg * (1.0 + a * (1.0 - sg))).astype(bf16)
        db = (dact * sa).astype(bf16)
        dh = dh + lax.dot_general(da, wg, contract, preferred_element_type=f32)
        dh = dh + lax.dot_general(db, wu, contract, preferred_element_type=f32)
    return dh, score


def shards(acts, cotangent, gain, router, ids, w_gate, w_up, w_down):
    ny, nx, nz, nc = (lax.axis_size(n) for n in ("y", "x", "z", "core"))
    y, x, core = (lax.axis_index(n) for n in ("y", "x", "core"))
    tokens, width = acts.shape
    top = ids.shape[1]
    experts = nz * nc
    cap = min(tokens, (17 * tokens * top + 16 * experts - 1) // (16 * experts))
    part = width // ny
    parity = x % 2
    own = core == parity

    mine = (w_gate[0], w_up[0], w_down[0])
    pairs = []
    for m in range(nx // 2):
        i, j = (2 * m) * nc + 1, (2 * m + 1) * nc
        pairs += [(i, j), (j, i)]
    swapped = tuple(lax.ppermute(w, ("x", "core"), pairs) for w in mine)
    first = tuple(jnp.where(own, w, s) for w, s in zip(mine, swapped))
    second = tuple(lax.ppermute(w, "core", [(0, 1), (1, 0)]) for w in first)

    h, sig, total, weight, select = token_weights(acts, gain, router, ids)
    names = 2 * jnp.arange(nz, dtype=jnp.int32) + parity
    here = slots(ids, names, cap)
    pick = here.astype(bf16).reshape(nz * cap, tokens)
    h_part = lax.dynamic_slice_in_dim(h, y * part, part, 1)
    g_part = lax.dynamic_slice_in_dim(cotangent, y * part, part, 1)
    both = jnp.concatenate([h_part, g_part], axis=1)
    rows = jnp.dot(pick, both, preferred_element_type=f32).astype(bf16)
    rows = lax.all_to_all(rows.reshape(nz, cap, 2 * part), "z", 0, 0, tiled=True)
    gathered = lax.all_gather(rows.reshape(nz * cap, 2 * part), "y")
    chosen = jnp.any(ids[:, :, None] == names[None, None, :], axis=1)
    of_name = (ids[:, :, None] == names[None, None, :]).astype(f32)
    dense = jnp.sum(of_name * weight[:, :, None], axis=1)
    gate = jnp.sum(here.astype(f32) * dense.T[:, None, :], axis=-1).astype(bf16)
    gate = lax.all_to_all(gate, "z", 0, 0, tiled=True).reshape(nz * cap, 1).astype(f32)

    h_rows = jnp.concatenate([gathered[i, :, :part] for i in range(ny)], axis=1)
    g_rows = jnp.concatenate([gathered[i, :, part:] for i in range(ny)], axis=1)
    dh, score = expert_rows(h_rows, g_rows, gate, (first, second))

    dh = dh.astype(bf16).reshape(nz * cap, ny, part).swapaxes(0, 1)
    dh = lax.psum_scatter(dh, "y", scatter_dimension=0)
    score = lax.all_to_all(score.reshape(nz, cap), "z", 0, 0, tiled=True)
    score = jnp.sum(here.astype(f32) * score[:, :, None], axis=1)
    score = jnp.sum(of_name * score.T[:, None, :], axis=-1)
    dh = lax.all_to_all(dh.reshape(nz, cap, part), "z", 0, 0, tiled=True)
    dh_tok = lax.dot_general(
        pick, dh.reshape(nz * cap, part), (((0,), (0,)), ((), ())), preferred_element_type=f32
    )
    sections = ny * nx
    share = tokens // sections
    tail = jnp.zeros((tokens, 128), f32).at[:, :top].set(score)
    packet = jnp.concatenate([dh_tok, tail], axis=1).reshape(sections, share, part + 128)
    packet = lax.all_to_all(packet, ("y", "x"), 0, 0, tiled=True)
    packet = packet.reshape(ny, nx, share, part + 128).sum(axis=1)
    dh_share = jnp.concatenate([packet[i, :, :part] for i in range(ny)], axis=1)
    score_share = packet[:, :, part : part + top].sum(axis=0)

    start = (y * nx + x) * share
    cut = lambda v: lax.dynamic_slice_in_dim(v, start, share, 0)
    sig, total, weight, select = cut(sig), cut(total), cut(weight), cut(select)
    wide = cut(acts).astype(f32)
    g = cut(cotangent).astype(f32)
    dsig = (score_share - jnp.sum(weight * score_share, axis=1, keepdims=True)) / total
    dpick = dsig * sig * (1.0 - sig)
    dlogits = jnp.sum(dpick[:, :, None] * select, axis=1)
    dh_total = dh_share + lax.dot_general(
        dlogits, router.astype(f32), (((1,), (1,)), ((), ())), precision=lax.Precision.HIGHEST
    )
    recip = lax.rsqrt(jnp.mean(wide * wide, axis=-1, keepdims=True) + eps)
    scaled = dh_total * gain
    pulled = recip * scaled - wide * (recip * recip * recip) * jnp.mean(
        wide * scaled, axis=-1, keepdims=True
    )
    return (g + pulled)[None]


def solution(mesh):
    pipe, expert = mesh.devices.shape
    grid = Mesh(
        mesh.devices.reshape(pipe // X, X, expert // CORES, CORES), ("y", "x", "z", "core")
    )
    exp, pipe = ("z", "core"), ("y", "x")
    in_specs = (
        P(exp, None),
        P(exp, None),
        P(),
        P(),
        P(exp, None),
        P(exp, None, pipe),
        P(exp, None, pipe),
        P(exp, pipe, None),
    )
    return jax.shard_map(
        shards, mesh=grid, in_specs=in_specs, out_specs=P(pipe, exp, None), check_vma=False
    )
```

```python
import functools
import jax
import jax.numpy as jnp
from jax import lax
from jax.experimental import pallas as pl
from jax.experimental.pallas import tpu as pltpu
from jax.sharding import Mesh, PartitionSpec as P

eps = 1e-05
X = 4
CORES = 2
bf16 = jnp.bfloat16
f32 = jnp.float32


def token_weights(acts, gain, router, ids):
    wide = acts.astype(f32)
    recip = lax.rsqrt(jnp.mean(wide * wide, axis=-1, keepdims=True) + eps)
    h = (wide * recip * gain).astype(bf16)
    logits = jnp.dot(h, router, preferred_element_type=f32)
    experts = router.shape[1]
    select = (ids[:, :, None] == jnp.arange(experts, dtype=jnp.int32)[None, None, :]).astype(f32)
    picked = jnp.sum(select * logits[:, None, :], axis=-1)
    sig = jax.nn.sigmoid(picked)
    total = jnp.sum(sig, axis=1, keepdims=True)
    return h, sig, total, sig / total, select


def slots(ids, names, cap, rank):
    tokens = ids.shape[0]
    member = jnp.any(ids[:, :, None] == names[None, None, :], axis=1)
    below = (jnp.arange(tokens)[:, None] > jnp.arange(tokens)[None, :]).astype(bf16)
    place = jnp.dot(below, member.astype(bf16), preferred_element_type=f32).astype(jnp.int32)
    place = jnp.where(member, place, rank)
    return place.T[:, None, :] == jnp.arange(rank, dtype=jnp.int32)[None, :, None]


def expert_kernel(cap, nz, rows_hbm, gate_ref, *refs):
    weights, (out_ref, rows, wg, wu, wd, sem) = refs[:6], refs[6:]
    ny, count, part = rows.shape[0], rows.shape[1], rows.shape[2] // 2
    rank = out_ref.shape[2]
    contract = (((1,), (1,)), ((), ()))
    copies = []
    for i in range(ny):
        band = pl.ds(i * part, part)
        mine = [(rows_hbm.at[i], rows.at[i])]
        for u in range(2):
            g_hbm, u_hbm, d_hbm = weights[3 * u : 3 * u + 3]
            mine.append((g_hbm.at[band, :], wg.at[u, band, :]))
            mine.append((u_hbm.at[band, :], wu.at[u, band, :]))
            mine.append((d_hbm.at[:, band], wd.at[u, :, band]))
        mine = [pltpu.make_async_copy(s, d, sem.at[i, j]) for j, (s, d) in enumerate(mine)]
        for copy in mine:
            copy.start()
        copies.append(mine)
    a, b, pulled = [0.0, 0.0], [0.0, 0.0], [0.0, 0.0]
    for i in range(ny):
        band = pl.ds(i * part, part)
        for copy in copies[i]:
            copy.wait()
        h = rows[i, :, :part]
        g = rows[i, :, part:]
        for u in range(2):
            a[u] = a[u] + jnp.dot(h, wg[u, band, :], preferred_element_type=f32)
            b[u] = b[u] + jnp.dot(h, wu[u, band, :], preferred_element_type=f32)
            pulled[u] = pulled[u] + lax.dot_general(
                g, wd[u, :, band], contract, preferred_element_type=f32
            )
    da, db = [], []
    score = 0.0
    gate = gate_ref[...]
    for u in range(2):
        sg = jax.nn.sigmoid(a[u])
        sa = a[u] * sg
        act = (sa * b[u]).astype(bf16).astype(f32)
        score = score + jnp.sum(act * pulled[u], axis=1, keepdims=True)
        dact = pulled[u] * gate
        da.append((dact * b[u] * sg * (1.0 + a[u] * (1.0 - sg))).astype(bf16))
        db.append((dact * sa).astype(bf16))
    lanes = lax.broadcasted_iota(jnp.int32, (cap, part), 1)
    eye = lanes == lax.broadcasted_iota(jnp.int32, (cap, part), 0)
    tails = []
    for z in range(nz):
        line = jnp.sum(jnp.where(eye, score[z * cap : (z + 1) * cap], 0.0), axis=0, keepdims=True)
        high = line.astype(bf16).astype(f32)
        rest = jnp.zeros((rank - cap - 2, part), f32)
        tails.append(jnp.concatenate([high, line - high, rest], axis=0))
    for i in range(ny):
        band = pl.ds(i * part, part)
        dh = 0.0
        for u in range(2):
            dh = dh + lax.dot_general(da[u], wg[u, band, :], contract, preferred_element_type=f32)
            dh = dh + lax.dot_general(db[u], wu[u, band, :], contract, preferred_element_type=f32)
        for z in range(nz):
            block = jnp.concatenate([dh[z * cap : (z + 1) * cap], tails[z]], axis=0)
            out_ref[i, z] = block.astype(bf16)


def expert_rows(gathered, gate, first, second, nz, cap, rank):
    ny, count, wide = gathered.shape
    hidden = first[0].shape[1]
    width = ny * wide // 2
    hbm = pl.BlockSpec(memory_space=pl.ANY)
    vmem = pl.BlockSpec(memory_space=pltpu.VMEM)
    return pl.pallas_call(
        functools.partial(expert_kernel, cap, nz),
        out_shape=jax.ShapeDtypeStruct((ny, nz, rank, wide // 2), bf16),
        in_specs=[hbm, vmem] + [hbm] * 6,
        out_specs=vmem,
        scratch_shapes=[
            pltpu.VMEM((ny, count, wide), bf16),
            pltpu.VMEM((2, width, hidden), bf16),
            pltpu.VMEM((2, width, hidden), bf16),
            pltpu.VMEM((2, hidden, width), bf16),
            pltpu.SemaphoreType.DMA((ny, 7)),
        ],
        compiler_params=pltpu.CompilerParams(vmem_limit_bytes=40 * 1024 * 1024),
        cost_estimate=pl.CostEstimate(
            flops=12 * count * width * hidden * 2,
            bytes_accessed=2 * (ny * count * wide + 6 * width * hidden + count * width),
            transcendentals=2 * count * hidden,
        ),
    )(gathered, gate, *first, *second)


def shards(acts, cotangent, gain, router, ids, w_gate, w_up, w_down):
    ny, nx, nz, nc = (lax.axis_size(n) for n in ("y", "x", "z", "core"))
    y, x, core = (lax.axis_index(n) for n in ("y", "x", "core"))
    tokens, width = acts.shape
    top = ids.shape[1]
    experts = nz * nc
    cap = min(tokens, (17 * tokens * top + 16 * experts - 1) // (16 * experts))
    part = width // ny
    parity = x % 2
    own = core == parity

    mine = (w_gate[0], w_up[0], w_down[0])
    pairs = []
    for m in range(nx // 2):
        i, j = (2 * m) * nc + 1, (2 * m + 1) * nc
        pairs += [(i, j), (j, i)]
    swapped = tuple(lax.ppermute(w, ("x", "core"), pairs) for w in mine)
    first = tuple(jnp.where(own, w, s) for w, s in zip(mine, swapped))
    second = tuple(lax.ppermute(w, "core", [(0, 1), (1, 0)]) for w in first)

    h, sig, total, weight, select = token_weights(acts, gain, router, ids)
    names = 2 * jnp.arange(nz, dtype=jnp.int32) + parity
    rank = -(-(cap + 2) // 8) * 8
    here = slots(ids, names, cap, rank)
    pick = here.astype(bf16)
    of_name = (ids[:, :, None] == names[None, None, :]).astype(f32)
    dense = jnp.sum(of_name * weight[:, :, None], axis=1)
    gate = jnp.sum(here.astype(f32) * dense.T[:, None, :], axis=-1).astype(bf16)
    h_part = lax.dynamic_slice_in_dim(h, y * part, part, 1)
    g_part = lax.dynamic_slice_in_dim(cotangent, y * part, part, 1)
    both = jnp.concatenate([h_part, g_part], axis=1)
    rows = jnp.dot(pick.reshape(nz * rank, tokens), both, preferred_element_type=f32)
    rows = rows.astype(bf16).reshape(nz, rank, 2 * part)
    line = jnp.pad(gate, ((0, 0), (0, 2 * part - rank)))[:, None, :]
    at_cap = (jnp.arange(rank) == cap)[None, :, None]
    rows = jnp.where(at_cap, line, rows)
    rows = lax.all_to_all(rows, "z", 0, 0, tiled=True)
    gathered = lax.all_gather(rows[:, :cap].reshape(nz * cap, 2 * part), "y")
    gate = rows[:, cap, :cap].astype(f32).reshape(nz * cap, 1)

    back = expert_rows(gathered, gate, first, second, nz, cap, rank)

    back = back.reshape(ny * nz, rank, part)
    back = lax.all_to_all(back, ("y", "z"), 0, 0, tiled=True)
    spread = jnp.broadcast_to(pick[None], (ny, nz, rank, tokens)).reshape(ny * nz * rank, tokens)
    dh_tok = lax.dot_general(
        spread,
        back.reshape(ny * nz * rank, part),
        (((0,), (0,)), ((), ())),
        preferred_element_type=f32,
    )
    score = jnp.sum(back[:, cap : cap + 2, :rank].astype(f32), axis=1)
    score = score.reshape(ny, nz, rank).sum(axis=0)
    score = jnp.sum(here.astype(f32) * score[:, :, None], axis=1)
    score = jnp.sum(of_name * score.T[:, None, :], axis=-1)
    sections = ny * nx
    share = tokens // sections
    tail = jnp.zeros((tokens, 128), f32).at[:, :top].set(score)
    packet = jnp.concatenate([dh_tok, tail], axis=1).reshape(sections, share, part + 128)
    packet = lax.all_to_all(packet, ("y", "x"), 0, 0, tiled=True)
    packet = packet.reshape(ny, nx, share, part + 128).sum(axis=1)
    dh_share = jnp.concatenate([packet[i, :, :part] for i in range(ny)], axis=1)
    score_share = packet[0, :, part : part + top]

    start = (y * nx + x) * share
    cut = lambda v: lax.dynamic_slice_in_dim(v, start, share, 0)
    sig, total, weight, select = cut(sig), cut(total), cut(weight), cut(select)
    wide = cut(acts).astype(f32)
    g = cut(cotangent).astype(f32)
    dsig = (score_share - jnp.sum(weight * score_share, axis=1, keepdims=True)) / total
    dpick = dsig * sig * (1.0 - sig)
    dlogits = jnp.sum(dpick[:, :, None] * select, axis=1)
    dh_total = dh_share + lax.dot_general(
        dlogits, router.astype(f32), (((1,), (1,)), ((), ())), precision=lax.Precision.HIGHEST
    )
    recip = lax.rsqrt(jnp.mean(wide * wide, axis=-1, keepdims=True) + eps)
    scaled = dh_total * gain
    pulled = recip * scaled - wide * (recip * recip * recip) * jnp.mean(
        wide * scaled, axis=-1, keepdims=True
    )
    return (g + pulled)[None]


def solution(mesh):
    pipe, expert = mesh.devices.shape
    grid = Mesh(
        mesh.devices.reshape(pipe // X, X, expert // CORES, CORES), ("y", "x", "z", "core")
    )
    exp, pipe = ("z", "core"), ("y", "x")
    in_specs = (
        P(exp, None),
        P(exp, None),
        P(),
        P(),
        P(exp, None),
        P(exp, None, pipe),
        P(exp, None, pipe),
        P(exp, pipe, None),
    )
    return jax.shard_map(
        shards, mesh=grid, in_specs=in_specs, out_specs=P(pipe, exp, None), check_vma=False
    )
```

```python
import functools
import jax
import jax.numpy as jnp
from jax import lax
from jax.experimental import pallas as pl
from jax.experimental.pallas import tpu as pltpu
from jax.sharding import Mesh, PartitionSpec as P

eps = 1e-05
X = 4
CORES = 2
LANE = 128
bf16 = jnp.bfloat16
f32 = jnp.float32


def token_weights(acts, gain, router, ids):
    wide = acts.astype(f32)
    recip = lax.rsqrt(jnp.mean(wide * wide, axis=-1, keepdims=True) + eps)
    h = (wide * recip * gain).astype(bf16)
    logits = jnp.dot(h, router, preferred_element_type=f32)
    experts = router.shape[1]
    select = (ids[:, :, None] == jnp.arange(experts, dtype=jnp.int32)[None, None, :]).astype(f32)
    picked = jnp.sum(select * logits[:, None, :], axis=-1)
    sig = jax.nn.sigmoid(picked)
    total = jnp.sum(sig, axis=1, keepdims=True)
    return h, sig, total, sig / total, select


def places(ids, names):
    tokens = ids.shape[0]
    member = jnp.any(ids[:, :, None] == names[None, None, :], axis=1)
    below = (jnp.arange(tokens)[:, None] > jnp.arange(tokens)[None, :]).astype(bf16)
    place = jnp.dot(below, member.astype(bf16), preferred_element_type=f32).astype(jnp.int32)
    return jnp.where(member, place, -4096).T


def at_rows(place, count):
    return place[:, None, :] == jnp.arange(count, dtype=jnp.int32)[None, :, None]


def expert_kernel(cap, nz, info, rows_hbm, mine, far, left, right, keep_ref, give_ref, *scratch):
    h_ref, g_ref, w_ref, row_sem, w_sem = scratch
    ny, groups, count = rows_hbm.shape[0], rows_hbm.shape[1], rows_hbm.shape[2]
    part = rows_hbm.shape[3] // 2
    rank, lane = keep_ref.shape[2], keep_ref.shape[3]
    pieces = part // lane
    contract = (((1,), (1,)), ((), ()))
    own, core = info[0], info[1]

    def fetch(u, source):
        return pltpu.make_async_copy(source, w_ref.at[u], w_sem.at[u])

    @pl.when(own == 1)
    def _():
        fetch(0, mine).start()

    @pl.when(own == 0)
    def _():
        fetch(0, left).start()

    row_copies = []
    for j, ref in enumerate((h_ref, g_ref)):
        for i in range(ny):
            for k in range(groups):
                from_core = core if k == 0 else 1 - core
                row_copies.append(
                    pltpu.make_async_copy(
                        rows_hbm.at[i, from_core, :, pl.ds(j * part, part)],
                        ref.at[pl.ds(k * count, count), pl.ds(i * part, part)],
                        row_sem.at[j, i, k],
                    )
                )
    for copy in row_copies:
        copy.start()

    @pl.when(own == 1)
    def _():
        fetch(1, far).start()

    @pl.when(own == 0)
    def _():
        fetch(1, right).start()

    for copy in row_copies:
        copy.wait()
    score = 0.0
    pulls = []
    for u in range(2):
        fetch(u, mine).wait()
        a = lax.dot_general(h_ref[...], w_ref[u, 0], contract, preferred_element_type=f32)
        b = lax.dot_general(h_ref[...], w_ref[u, 1], contract, preferred_element_type=f32)
        dact = lax.dot_general(g_ref[...], w_ref[u, 2], contract, preferred_element_type=f32)
        sg = jax.nn.sigmoid(a)
        sa = a * sg
        act = (sa * b).astype(bf16).astype(f32)
        score = score + jnp.sum(act * dact, axis=1, keepdims=True)
        pulls.append((dact * b * sg * (1.0 + a * (1.0 - sg))).astype(bf16))
        pulls.append((dact * sa).astype(bf16))
    lanes = lax.broadcasted_iota(jnp.int32, (cap, lane), 1)
    eye = lanes == lax.broadcasted_iota(jnp.int32, (cap, lane), 0)
    gap = jnp.zeros((2, lane), f32)
    rest = jnp.zeros((rank - pieces * cap - 4, lane), f32)
    tails = []
    for k in range(groups):
        for z in range(nz):
            first = k * count + z * cap
            line = jnp.sum(jnp.where(eye, score[first : first + cap], 0.0), axis=0, keepdims=True)
            high = line.astype(bf16).astype(f32)
            pair = [high, line - high]
            tails.append(pair + [gap, rest] if k == 0 else [gap] + pair + [rest])
    for i in range(ny):
        band = pl.ds(i * part, part)
        dh = 0.0
        for u in range(2):
            for j in range(2):
                dh = dh + jnp.dot(pulls[2 * u + j], w_ref[u, j, :, band], preferred_element_type=f32)
        for k, ref in enumerate((keep_ref, give_ref)):
            for z in range(nz):
                first = k * count + z * cap
                block = dh[first : first + cap]
                block = [block[:, p * lane : (p + 1) * lane] for p in range(pieces)]
                block = jnp.concatenate(block + tails[k * nz + z], axis=0)
                ref[i, z] = block.astype(ref.dtype)


def expert_rows(info, gathered, slices, nz, cap, rank):
    ny, groups, count, wide = gathered.shape
    kinds, hidden, width = slices[0].shape
    hbm = pl.BlockSpec(memory_space=pl.ANY)
    vmem = pl.BlockSpec(memory_space=pltpu.VMEM)
    rows = groups * count
    return pl.pallas_call(
        functools.partial(expert_kernel, cap, nz),
        out_shape=(
            jax.ShapeDtypeStruct((ny, nz, rank, LANE), f32),
            jax.ShapeDtypeStruct((ny, nz, rank, LANE), bf16),
        ),
        in_specs=[pl.BlockSpec(memory_space=pltpu.SMEM)] + [hbm] * 5,
        out_specs=(vmem, vmem),
        scratch_shapes=[
            pltpu.VMEM((rows, width), bf16),
            pltpu.VMEM((rows, width), bf16),
            pltpu.VMEM((2, kinds, hidden, width), bf16),
            pltpu.SemaphoreType.DMA((2, ny, groups)),
            pltpu.SemaphoreType.DMA((2,)),
        ],
        compiler_params=pltpu.CompilerParams(vmem_limit_bytes=56 * 1024 * 1024),
        cost_estimate=pl.CostEstimate(
            flops=20 * rows * width * hidden,
            bytes_accessed=2 * (2 * rows * width + 6 * width * hidden + 2 * rows * width),
            transcendentals=2 * rows * hidden,
        ),
    )(info, gathered, *slices)


def shards(acts, cotangent, gain, router, ids, w_gate, w_up, w_down):
    ny, nx, nz, nc = (lax.axis_size(n) for n in ("y", "x", "z", "core"))
    y, x, core = (lax.axis_index(n) for n in ("y", "x", "core"))
    tokens, width = acts.shape
    top = ids.shape[1]
    experts = nz * nc
    cap = min(tokens, (17 * tokens * top + 16 * experts - 1) // (16 * experts))
    cap = -(-cap // 2)
    part = width // ny
    parity = x % 2

    mine = jnp.stack([w_gate[0].T, w_up[0].T, w_down[0]])
    ahead, behind, across = [], [], []
    for i in range(nx):
        a = i % 2
        ahead.append((i * nc + 1 - a, (i + 1) % nx * nc + a))
        behind.append((i * nc + 1 - a, (i - 1) % nx * nc + a))
        across.append((i * nc + a, (i + 2) % nx * nc + a))
    left = lax.ppermute(mine, ("x", "core"), behind)
    right = lax.ppermute(mine, ("x", "core"), ahead)
    info = jnp.stack([(core == parity).astype(jnp.int32), core.astype(jnp.int32)])

    h, sig, total, weight, select = token_weights(acts, gain, router, ids)
    names = 2 * jnp.arange(nz, dtype=jnp.int32) + parity
    place = places(ids, names) - x // 2 * cap
    place = jnp.where((place >= 0) & (place < cap), place, -4096)
    here = at_rows(place, cap)
    of_name = (ids[:, :, None] == names[None, None, :]).astype(f32)
    dense = jnp.sum(of_name * weight[:, :, None], axis=1).astype(bf16)
    h_part = lax.dynamic_slice_in_dim(h, y * part, part, 1)
    g_part = lax.dynamic_slice_in_dim(cotangent, y * part, part, 1)
    rank = -(-cap // 8) * 8
    pick = at_rows(place, rank).astype(bf16)
    scaled = pick * dense.T[:, None, :]
    h_rows = jnp.dot(pick.reshape(nz * rank, tokens), h_part, preferred_element_type=f32)
    dy_rows = jnp.dot(scaled.reshape(nz * rank, tokens), g_part, preferred_element_type=f32)
    rows = jnp.concatenate([h_rows.astype(bf16), dy_rows.astype(bf16)], axis=1)
    rows = lax.all_to_all(rows.reshape(nz, rank, 2 * part), "z", 0, 0, tiled=True)
    count = -(-nz * cap // 16) * 16
    rows = rows[:, :cap].reshape(nz * cap, 2 * part)
    rows = jnp.pad(rows, ((0, count - nz * cap), (0, 0)))
    gathered = lax.all_gather(rows, ("y", "core"), tiled=True)
    left, right, source, _ = lax.optimization_barrier((left, right, mine, rows))
    far = lax.ppermute(source, ("x", "core"), across)

    pieces = part // LANE
    rank = -(-(pieces * cap + 4) // 8) * 8
    keep, give = expert_rows(
        info, gathered.reshape(ny, nc, count, 2 * part), (mine, far, left, right), nz, cap, rank
    )
    got = lax.ppermute(give, "core", [(0, 1), (1, 0)])
    back = (keep + got.astype(f32)).astype(bf16)

    back = lax.all_to_all(back.reshape(ny * nz, rank, LANE), ("y", "z"), 0, 0, tiled=True)
    flat = back.reshape(ny * nz * rank, LANE)
    parts = []
    for k in range(pieces):
        spread = at_rows(place + k * cap, rank).astype(bf16)
        spread = jnp.broadcast_to(spread[None], (ny, nz, rank, tokens))
        parts.append(
            lax.dot_general(
                spread.reshape(ny * nz * rank, tokens),
                flat,
                (((0,), (0,)), ((), ())),
                preferred_element_type=f32,
            )
        )
    score = jnp.sum(back[:, pieces * cap : pieces * cap + 4, :cap].astype(f32), axis=1)
    score = score.reshape(ny, nz, cap).sum(axis=0)
    score = jnp.sum(here.astype(f32) * score[:, :, None], axis=1)
    score = jnp.sum(of_name * score.T[:, None, :], axis=-1)
    sections = ny * nx
    share = tokens // sections
    tail = jnp.zeros((tokens, LANE), f32).at[:, :top].set(score)
    packet = jnp.concatenate(parts + [tail], axis=1).reshape(sections, share, part + LANE)
    packet = lax.all_to_all(packet, ("y", "x"), 0, 0, tiled=True)
    packet = packet.reshape(ny, nx, share, part + LANE).sum(axis=1)
    dh_share = jnp.concatenate([packet[i, :, :part] for i in range(ny)], axis=1)
    score_share = packet[0, :, part : part + top]

    start = (y * nx + x) * share
    cut = lambda v: lax.dynamic_slice_in_dim(v, start, share, 0)
    sig, total, weight, select = cut(sig), cut(total), cut(weight), cut(select)
    wide = cut(acts).astype(f32)
    g = cut(cotangent).astype(f32)
    sent = weight.astype(bf16).astype(f32)
    score_share = jnp.where(sent > 0.0, score_share / jnp.where(sent > 0.0, sent, 1.0), 0.0)
    dsig = (score_share - jnp.sum(weight * score_share, axis=1, keepdims=True)) / total
    dpick = dsig * sig * (1.0 - sig)
    dlogits = jnp.sum(dpick[:, :, None] * select, axis=1)
    dh_total = dh_share + lax.dot_general(
        dlogits, router.astype(f32), (((1,), (1,)), ((), ())), precision=lax.Precision.HIGHEST
    )
    recip = lax.rsqrt(jnp.mean(wide * wide, axis=-1, keepdims=True) + eps)
    scaled = dh_total * gain
    pulled = recip * scaled - wide * (recip * recip * recip) * jnp.mean(
        wide * scaled, axis=-1, keepdims=True
    )
    return (g + pulled)[None]


def solution(mesh):
    pipe, expert = mesh.devices.shape
    grid = Mesh(
        mesh.devices.reshape(pipe // X, X, expert // CORES, CORES), ("y", "x", "z", "core")
    )
    exp, pipe = ("z", "core"), ("y", "x")
    in_specs = (
        P(exp, None),
        P(exp, None),
        P(),
        P(),
        P(exp, None),
        P(exp, None, pipe),
        P(exp, None, pipe),
        P(exp, pipe, None),
    )
    return jax.shard_map(
        shards, mesh=grid, in_specs=in_specs, out_specs=P(pipe, exp, None), check_vma=False
    )
```

```python
import functools
import jax
import jax.numpy as jnp
from jax import lax
from jax.experimental import pallas as pl
from jax.experimental.pallas import tpu as pltpu
from jax.sharding import Mesh, PartitionSpec as P

eps = 1e-05
X = 4
CORES = 2
LANE = 128
bf16 = jnp.bfloat16
f32 = jnp.float32


def token_weights(acts, gain, router, ids):
    wide = acts.astype(f32)
    recip = lax.rsqrt(jnp.mean(wide * wide, axis=-1, keepdims=True) + eps)
    h = (wide * recip * gain).astype(bf16)
    logits = jnp.dot(h, router, preferred_element_type=f32)
    experts = router.shape[1]
    select = (ids[:, :, None] == jnp.arange(experts, dtype=jnp.int32)[None, None, :]).astype(f32)
    picked = jnp.sum(select * logits[:, None, :], axis=-1)
    sig = jax.nn.sigmoid(picked)
    total = jnp.sum(sig, axis=1, keepdims=True)
    return h, sig, total, sig / total, select


def places(ids, names):
    tokens = ids.shape[0]
    member = jnp.any(ids[:, :, None] == names[None, None, :], axis=1)
    below = (jnp.arange(tokens)[:, None] > jnp.arange(tokens)[None, :]).astype(bf16)
    place = jnp.dot(below, member.astype(bf16), preferred_element_type=f32).astype(jnp.int32)
    return jnp.where(member, place, -4096).T


def at_rows(place, count):
    return place[:, None, :] == jnp.arange(count, dtype=jnp.int32)[None, :, None]


def expert_kernel(cap, nz, info, rows_hbm, *refs):
    slices, (left, right, keep_ref, give_ref) = refs[:6], refs[6:10]
    h_ref, g_ref, w_ref, row_sem, w_sem = refs[10:]
    ny, groups, count = rows_hbm.shape[0], rows_hbm.shape[1], rows_hbm.shape[2]
    part = rows_hbm.shape[3] // 2
    rank, lane = keep_ref.shape[2], keep_ref.shape[3]
    pieces = part // lane
    contract = (((1,), (1,)), ((), ()))
    own, core = info[0], info[1]

    def fetch(u):
        return [
            pltpu.make_async_copy(slices[3 * u + j], w_ref.at[u, j], w_sem.at[u, j])
            for j in range(3)
        ]

    def start(u, other):
        @pl.when(own == 1)
        def _():
            for copy in fetch(u):
                copy.start()

        @pl.when(own == 0)
        def _():
            for j in range(3):
                pltpu.make_async_copy(other.at[j], w_ref.at[u, j], w_sem.at[u, j]).start()

    start(0, left)

    row_copies = []
    for j, ref in enumerate((h_ref, g_ref)):
        for i in range(ny):
            for k in range(groups):
                from_core = core if k == 0 else 1 - core
                row_copies.append(
                    pltpu.make_async_copy(
                        rows_hbm.at[i, from_core, :, pl.ds(j * part, part)],
                        ref.at[pl.ds(k * count, count), pl.ds(i * part, part)],
                        row_sem.at[j, i, k],
                    )
                )
    for copy in row_copies:
        copy.start()
    start(1, right)
    for copy in row_copies:
        copy.wait()
    score = 0.0
    pulls = []
    for u in range(2):
        for copy in fetch(u):
            copy.wait()
        a = lax.dot_general(h_ref[...], w_ref[u, 0], contract, preferred_element_type=f32)
        b = lax.dot_general(h_ref[...], w_ref[u, 1], contract, preferred_element_type=f32)
        dact = lax.dot_general(g_ref[...], w_ref[u, 2], contract, preferred_element_type=f32)
        sg = jax.nn.sigmoid(a)
        sa = a * sg
        act = (sa * b).astype(bf16).astype(f32)
        score = score + jnp.sum(act * dact, axis=1, keepdims=True)
        pulls.append((dact * b * sg * (1.0 + a * (1.0 - sg))).astype(bf16))
        pulls.append((dact * sa).astype(bf16))
    lanes = lax.broadcasted_iota(jnp.int32, (cap, lane), 1)
    eye = lanes == lax.broadcasted_iota(jnp.int32, (cap, lane), 0)
    gap = jnp.zeros((2, lane), f32)
    rest = jnp.zeros((rank - pieces * cap - 4, lane), f32)
    tails = []
    for k in range(groups):
        for z in range(nz):
            first = k * count + z * cap
            line = jnp.sum(jnp.where(eye, score[first : first + cap], 0.0), axis=0, keepdims=True)
            high = line.astype(bf16).astype(f32)
            pair = [high, line - high]
            tails.append(pair + [gap, rest] if k == 0 else [gap] + pair + [rest])
    for i in range(ny):
        band = pl.ds(i * part, part)
        dh = 0.0
        for u in range(2):
            for j in range(2):
                dh = dh + jnp.dot(pulls[2 * u + j], w_ref[u, j, :, band], preferred_element_type=f32)
        for k, ref in enumerate((keep_ref, give_ref)):
            for z in range(nz):
                first = k * count + z * cap
                block = dh[first : first + cap]
                block = [block[:, p * lane : (p + 1) * lane] for p in range(pieces)]
                block = jnp.concatenate(block + tails[k * nz + z], axis=0)
                ref[i, z] = block.astype(ref.dtype)


def expert_rows(info, gathered, slices, nz, cap, rank):
    ny, groups, count, wide = gathered.shape
    kinds, hidden, width = slices[-1].shape
    hbm = pl.BlockSpec(memory_space=pl.ANY)
    vmem = pl.BlockSpec(memory_space=pltpu.VMEM)
    rows = groups * count
    return pl.pallas_call(
        functools.partial(expert_kernel, cap, nz),
        out_shape=(
            jax.ShapeDtypeStruct((ny, nz, rank, LANE), f32),
            jax.ShapeDtypeStruct((ny, nz, rank, LANE), bf16),
        ),
        in_specs=[pl.BlockSpec(memory_space=pltpu.SMEM)] + [hbm] * 9,
        out_specs=(vmem, vmem),
        scratch_shapes=[
            pltpu.VMEM((rows, width), bf16),
            pltpu.VMEM((rows, width), bf16),
            pltpu.VMEM((2, kinds, hidden, width), bf16),
            pltpu.SemaphoreType.DMA((2, ny, groups)),
            pltpu.SemaphoreType.DMA((2, 3)),
        ],
        compiler_params=pltpu.CompilerParams(vmem_limit_bytes=56 * 1024 * 1024),
        cost_estimate=pl.CostEstimate(
            flops=20 * rows * width * hidden,
            bytes_accessed=2 * (2 * rows * width + 6 * width * hidden + 2 * rows * width),
            transcendentals=2 * rows * hidden,
        ),
    )(info, gathered, *slices)


def shards(acts, cotangent, gain, router, ids, w_gate, w_up, w_down):
    ny, nx, nz, nc = (lax.axis_size(n) for n in ("y", "x", "z", "core"))
    y, x, core = (lax.axis_index(n) for n in ("y", "x", "core"))
    tokens, width = acts.shape
    top = ids.shape[1]
    experts = nz * nc
    cap = min(tokens, (17 * tokens * top + 16 * experts - 1) // (16 * experts))
    cap = -(-cap // 2)
    part = width // ny
    parity = x % 2

    own_slice = (w_gate[0].T, w_up[0].T, w_down[0])
    mine = jnp.stack(own_slice)
    ahead, behind, across = [], [], []
    for i in range(nx):
        a = i % 2
        ahead.append((i * nc + 1 - a, (i + 1) % nx * nc + a))
        behind.append((i * nc + 1 - a, (i - 1) % nx * nc + a))
        across.append((i * nc + a, (i + 2) % nx * nc + a))
    left = lax.ppermute(mine, ("x", "core"), behind)
    right = lax.ppermute(mine, ("x", "core"), ahead)
    info = jnp.stack([(core == parity).astype(jnp.int32), core.astype(jnp.int32)])

    h, sig, total, weight, select = token_weights(acts, gain, router, ids)
    names = 2 * jnp.arange(nz, dtype=jnp.int32) + parity
    place = places(ids, names) - x // 2 * cap
    place = jnp.where((place >= 0) & (place < cap), place, -4096)
    here = at_rows(place, cap)
    of_name = (ids[:, :, None] == names[None, None, :]).astype(f32)
    dense = jnp.sum(of_name * weight[:, :, None], axis=1).astype(bf16)
    h_part = lax.dynamic_slice_in_dim(h, y * part, part, 1)
    g_part = lax.dynamic_slice_in_dim(cotangent, y * part, part, 1)
    rank = -(-cap // 8) * 8
    pick = at_rows(place, rank).astype(bf16)
    scaled = pick * dense.T[:, None, :]
    h_rows = jnp.dot(pick.reshape(nz * rank, tokens), h_part, preferred_element_type=f32)
    dy_rows = jnp.dot(scaled.reshape(nz * rank, tokens), g_part, preferred_element_type=f32)
    rows = jnp.concatenate([h_rows.astype(bf16), dy_rows.astype(bf16)], axis=1)
    rows = lax.all_to_all(rows.reshape(nz, rank, 2 * part), "z", 0, 0, tiled=True)
    count = -(-nz * cap // 16) * 16
    rows = rows[:, :cap].reshape(nz * cap, 2 * part)
    rows = jnp.pad(rows, ((0, count - nz * cap), (0, 0)))
    gathered = lax.all_gather(rows, ("y", "core"), tiled=True)
    left, right, source, _ = lax.optimization_barrier((left, right, mine, rows))
    far = []
    for i in range(3):
        far.append(lax.ppermute(source[i], ("x", "core"), across))
        far[i], source = lax.optimization_barrier((far[i], source))

    pieces = part // LANE
    rank = -(-(pieces * cap + 4) // 8) * 8
    keep, give = expert_rows(
        info, gathered.reshape(ny, nc, count, 2 * part), (*own_slice, *far, left, right), nz, cap, rank
    )
    got = lax.ppermute(give, "core", [(0, 1), (1, 0)])
    back = (keep + got.astype(f32)).astype(bf16)

    back = lax.all_to_all(back.reshape(ny * nz, rank, LANE), ("y", "z"), 0, 0, tiled=True)
    flat = back.reshape(ny * nz * rank, LANE)
    parts = []
    for k in range(pieces):
        spread = at_rows(place + k * cap, rank).astype(bf16)
        spread = jnp.broadcast_to(spread[None], (ny, nz, rank, tokens))
        parts.append(
            lax.dot_general(
                spread.reshape(ny * nz * rank, tokens),
                flat,
                (((0,), (0,)), ((), ())),
                preferred_element_type=f32,
            )
        )
    score = jnp.sum(back[:, pieces * cap : pieces * cap + 4, :cap].astype(f32), axis=1)
    score = score.reshape(ny, nz, cap).sum(axis=0)
    score = jnp.sum(here.astype(f32) * score[:, :, None], axis=1)
    score = jnp.sum(of_name * score.T[:, None, :], axis=-1)
    sections = ny * nx
    share = tokens // sections
    tail = jnp.zeros((tokens, LANE), f32).at[:, :top].set(score)
    packet = jnp.concatenate(parts + [tail], axis=1).reshape(sections, share, part + LANE)
    packet = lax.all_to_all(packet, ("y", "x"), 0, 0, tiled=True)
    packet = packet.reshape(ny, nx, share, part + LANE).sum(axis=1)
    dh_share = jnp.concatenate([packet[i, :, :part] for i in range(ny)], axis=1)
    score_share = packet[0, :, part : part + top]

    start = (y * nx + x) * share
    cut = lambda v: lax.dynamic_slice_in_dim(v, start, share, 0)
    sig, total, weight, select = cut(sig), cut(total), cut(weight), cut(select)
    wide = cut(acts).astype(f32)
    g = cut(cotangent).astype(f32)
    sent = weight.astype(bf16).astype(f32)
    score_share = jnp.where(sent > 0.0, score_share / jnp.where(sent > 0.0, sent, 1.0), 0.0)
    dsig = (score_share - jnp.sum(weight * score_share, axis=1, keepdims=True)) / total
    dpick = dsig * sig * (1.0 - sig)
    dlogits = jnp.sum(dpick[:, :, None] * select, axis=1)
    dh_total = dh_share + lax.dot_general(
        dlogits, router.astype(f32), (((1,), (1,)), ((), ())), precision=lax.Precision.HIGHEST
    )
    recip = lax.rsqrt(jnp.mean(wide * wide, axis=-1, keepdims=True) + eps)
    scaled = dh_total * gain
    pulled = recip * scaled - wide * (recip * recip * recip) * jnp.mean(
        wide * scaled, axis=-1, keepdims=True
    )
    return (g + pulled)[None]


def solution(mesh):
    pipe, expert = mesh.devices.shape
    grid = Mesh(
        mesh.devices.reshape(pipe // X, X, expert // CORES, CORES), ("y", "x", "z", "core")
    )
    exp, pipe = ("z", "core"), ("y", "x")
    in_specs = (
        P(exp, None),
        P(exp, None),
        P(),
        P(),
        P(exp, None),
        P(exp, None, pipe),
        P(exp, None, pipe),
        P(exp, pipe, None),
    )
    return jax.shard_map(
        shards, mesh=grid, in_specs=in_specs, out_specs=P(pipe, exp, None), check_vma=False
    )
```

```python
import functools
import jax
import jax.numpy as jnp
from jax import lax
from jax.experimental import pallas as pl
from jax.experimental.pallas import tpu as pltpu
from jax.sharding import Mesh, PartitionSpec as P

eps = 1e-05
X = 4
CORES = 2
LANE = 128
bf16 = jnp.bfloat16
f32 = jnp.float32


def token_weights(acts, gain, router, ids):
    wide = acts.astype(f32)
    recip = lax.rsqrt(jnp.mean(wide * wide, axis=-1, keepdims=True) + eps)
    h = (wide * recip * gain).astype(bf16)
    logits = jnp.dot(h, router, preferred_element_type=f32)
    experts = router.shape[1]
    select = (ids[:, :, None] == jnp.arange(experts, dtype=jnp.int32)[None, None, :]).astype(f32)
    picked = jnp.sum(select * logits[:, None, :], axis=-1)
    sig = jax.nn.sigmoid(picked)
    total = jnp.sum(sig, axis=1, keepdims=True)
    return h, sig, total, sig / total, select


def places(ids, names):
    tokens = ids.shape[0]
    member = jnp.any(ids[:, :, None] == names[None, None, :], axis=1)
    below = (jnp.arange(tokens)[:, None] > jnp.arange(tokens)[None, :]).astype(bf16)
    place = jnp.dot(below, member.astype(bf16), preferred_element_type=f32).astype(jnp.int32)
    return jnp.where(member, place, -4096).T


def at_rows(place, count):
    return place[:, None, :] == jnp.arange(count, dtype=jnp.int32)[None, :, None]


def expert_kernel(cap, nz, info, rows_hbm, *refs):
    mine, (far, left, right, keep_ref, give_ref) = refs[:3], refs[3:8]
    h_ref, g_ref, w_ref, row_sem, w_sem = refs[8:]
    ny, groups, count = rows_hbm.shape[0], rows_hbm.shape[1], rows_hbm.shape[2]
    part = rows_hbm.shape[3] // 2
    rank, lane = keep_ref.shape[2], keep_ref.shape[3]
    pieces = part // lane
    contract = (((1,), (1,)), ((), ()))
    own, core = info[0], info[1]

    def fetch(u, source):
        return [pltpu.make_async_copy(source[j], w_ref.at[u, j], w_sem.at[u, j]) for j in range(3)]

    def start(u, if_own, other):
        @pl.when(own == 1)
        def _():
            for copy in fetch(u, if_own):
                copy.start()

        @pl.when(own == 0)
        def _():
            for copy in fetch(u, other):
                copy.start()

    left, right, far = ([ref.at[j] for j in range(3)] for ref in (left, right, far))
    start(0, mine, left)

    row_copies = []
    for j, ref in enumerate((h_ref, g_ref)):
        for i in range(ny):
            for k in range(groups):
                from_core = core if k == 0 else 1 - core
                row_copies.append(
                    pltpu.make_async_copy(
                        rows_hbm.at[i, from_core, :, pl.ds(j * part, part)],
                        ref.at[pl.ds(k * count, count), pl.ds(i * part, part)],
                        row_sem.at[j, i, k],
                    )
                )
    for copy in row_copies:
        copy.start()
    start(1, far, right)
    for copy in row_copies:
        copy.wait()
    score = 0.0
    pulls = []
    for u in range(2):
        for copy in fetch(u, mine):
            copy.wait()
        a = lax.dot_general(h_ref[...], w_ref[u, 0], contract, preferred_element_type=f32)
        b = lax.dot_general(h_ref[...], w_ref[u, 1], contract, preferred_element_type=f32)
        dact = lax.dot_general(g_ref[...], w_ref[u, 2], contract, preferred_element_type=f32)
        sg = jax.nn.sigmoid(a)
        sa = a * sg
        act = (sa * b).astype(bf16).astype(f32)
        score = score + jnp.sum(act * dact, axis=1, keepdims=True)
        pulls.append((dact * b * sg * (1.0 + a * (1.0 - sg))).astype(bf16))
        pulls.append((dact * sa).astype(bf16))
    lanes = lax.broadcasted_iota(jnp.int32, (cap, lane), 1)
    eye = lanes == lax.broadcasted_iota(jnp.int32, (cap, lane), 0)
    gap = jnp.zeros((2, lane), f32)
    rest = jnp.zeros((rank - pieces * cap - 4, lane), f32)
    tails = []
    for k in range(groups):
        for z in range(nz):
            first = k * count + z * cap
            line = jnp.sum(jnp.where(eye, score[first : first + cap], 0.0), axis=0, keepdims=True)
            high = line.astype(bf16).astype(f32)
            pair = [high, line - high]
            tails.append(pair + [gap, rest] if k == 0 else [gap] + pair + [rest])
    for i in range(ny):
        band = pl.ds(i * part, part)
        dh = 0.0
        for u in range(2):
            for j in range(2):
                dh = dh + jnp.dot(pulls[2 * u + j], w_ref[u, j, :, band], preferred_element_type=f32)
        for k, ref in enumerate((keep_ref, give_ref)):
            for z in range(nz):
                first = k * count + z * cap
                block = dh[first : first + cap]
                block = [block[:, p * lane : (p + 1) * lane] for p in range(pieces)]
                block = jnp.concatenate(block + tails[k * nz + z], axis=0)
                ref[i, z] = block.astype(ref.dtype)


def after_kernel(info, left, right, far, out):
    out[0] = info[0]
    out[1] = info[1]


def after(info, left, right, far):
    smem = pl.BlockSpec(memory_space=pltpu.SMEM)
    return pl.pallas_call(
        after_kernel,
        out_shape=jax.ShapeDtypeStruct(info.shape, info.dtype),
        in_specs=[smem] + [pl.BlockSpec(memory_space=pl.ANY)] * 3,
        out_specs=smem,
        cost_estimate=pl.CostEstimate(flops=50000000000, bytes_accessed=0, transcendentals=0),
    )(info, left, right, far)


def expert_rows(info, gathered, slices, nz, cap, rank):
    ny, groups, count, wide = gathered.shape
    kinds, hidden, width = slices[-1].shape
    hbm = pl.BlockSpec(memory_space=pl.ANY)
    vmem = pl.BlockSpec(memory_space=pltpu.VMEM)
    rows = groups * count
    return pl.pallas_call(
        functools.partial(expert_kernel, cap, nz),
        out_shape=(
            jax.ShapeDtypeStruct((ny, nz, rank, LANE), f32),
            jax.ShapeDtypeStruct((ny, nz, rank, LANE), bf16),
        ),
        in_specs=[pl.BlockSpec(memory_space=pltpu.SMEM)] + [hbm] * 7,
        out_specs=(vmem, vmem),
        scratch_shapes=[
            pltpu.VMEM((rows, width), bf16),
            pltpu.VMEM((rows, width), bf16),
            pltpu.VMEM((2, kinds, hidden, width), bf16),
            pltpu.SemaphoreType.DMA((2, ny, groups)),
            pltpu.SemaphoreType.DMA((2, 3)),
        ],
        compiler_params=pltpu.CompilerParams(vmem_limit_bytes=56 * 1024 * 1024),
        cost_estimate=pl.CostEstimate(
            flops=20 * rows * width * hidden,
            bytes_accessed=2 * (2 * rows * width + 6 * width * hidden + 2 * rows * width),
            transcendentals=2 * rows * hidden,
        ),
    )(info, gathered, *slices)


def shards(acts, cotangent, gain, router, ids, w_gate, w_up, w_down):
    ny, nx, nz, nc = (lax.axis_size(n) for n in ("y", "x", "z", "core"))
    y, x, core = (lax.axis_index(n) for n in ("y", "x", "core"))
    tokens, width = acts.shape
    top = ids.shape[1]
    experts = nz * nc
    cap = min(tokens, (17 * tokens * top + 16 * experts - 1) // (16 * experts))
    cap = -(-cap // 2)
    part = width // ny
    parity = x % 2

    own_slice = (w_gate[0].T, w_up[0].T, w_down[0])
    mine = jnp.stack(own_slice)
    ahead, behind, across = [], [], []
    for i in range(nx):
        a = i % 2
        ahead.append((i * nc + 1 - a, (i + 1) % nx * nc + a))
        behind.append((i * nc + 1 - a, (i - 1) % nx * nc + a))
        across.append((i * nc + a, (i + 2) % nx * nc + a))
    left = lax.ppermute(mine, ("x", "core"), behind)
    right = lax.ppermute(mine, ("x", "core"), ahead)
    far = lax.ppermute(mine, ("x", "core"), across)
    info = jnp.stack([(core == parity).astype(jnp.int32), core.astype(jnp.int32)])

    h, sig, total, weight, select = token_weights(acts, gain, router, ids)
    names = 2 * jnp.arange(nz, dtype=jnp.int32) + parity
    place = places(ids, names) - x // 2 * cap
    place = jnp.where((place >= 0) & (place < cap), place, -4096)
    here = at_rows(place, cap)
    of_name = (ids[:, :, None] == names[None, None, :]).astype(f32)
    dense = jnp.sum(of_name * weight[:, :, None], axis=1).astype(bf16)
    h_part = lax.dynamic_slice_in_dim(h, y * part, part, 1)
    g_part = lax.dynamic_slice_in_dim(cotangent, y * part, part, 1)
    rank = -(-cap // 8) * 8
    pick = at_rows(place, rank).astype(bf16)
    scaled = pick * dense.T[:, None, :]
    h_rows = jnp.dot(pick.reshape(nz * rank, tokens), h_part, preferred_element_type=f32)
    dy_rows = jnp.dot(scaled.reshape(nz * rank, tokens), g_part, preferred_element_type=f32)
    rows = jnp.concatenate([h_rows.astype(bf16), dy_rows.astype(bf16)], axis=1)
    rows = lax.all_to_all(rows.reshape(nz, rank, 2 * part), "z", 0, 0, tiled=True)
    count = -(-nz * cap // 16) * 16
    rows = rows[:, :cap].reshape(nz * cap, 2 * part)
    rows = jnp.pad(rows, ((0, count - nz * cap), (0, 0)))
    gathered = lax.all_gather(rows, ("y", "core"), tiled=True)
    info = after(info, left, right, far)

    pieces = part // LANE
    rank = -(-(pieces * cap + 4) // 8) * 8
    keep, give = expert_rows(
        info, gathered.reshape(ny, nc, count, 2 * part), (*own_slice, far, left, right), nz, cap, rank
    )
    got = lax.ppermute(give, "core", [(0, 1), (1, 0)])
    back = (keep + got.astype(f32)).astype(bf16)

    back = lax.all_to_all(back.reshape(ny * nz, rank, LANE), ("y", "z"), 0, 0, tiled=True)
    flat = back.reshape(ny * nz * rank, LANE)
    parts = []
    for k in range(pieces):
        spread = at_rows(place + k * cap, rank).astype(bf16)
        spread = jnp.broadcast_to(spread[None], (ny, nz, rank, tokens))
        parts.append(
            lax.dot_general(
                spread.reshape(ny * nz * rank, tokens),
                flat,
                (((0,), (0,)), ((), ())),
                preferred_element_type=f32,
            )
        )
    score = jnp.sum(back[:, pieces * cap : pieces * cap + 4, :cap].astype(f32), axis=1)
    score = score.reshape(ny, nz, cap).sum(axis=0)
    score = jnp.sum(here.astype(f32) * score[:, :, None], axis=1)
    score = jnp.sum(of_name * score.T[:, None, :], axis=-1)
    sections = ny * nx
    share = tokens // sections
    tail = jnp.zeros((tokens, LANE), f32).at[:, :top].set(score)
    packet = jnp.concatenate(parts + [tail], axis=1).reshape(sections, share, part + LANE)
    packet = lax.all_to_all(packet, ("y", "x"), 0, 0, tiled=True)
    packet = packet.reshape(ny, nx, share, part + LANE).sum(axis=1)
    dh_share = jnp.concatenate([packet[i, :, :part] for i in range(ny)], axis=1)
    score_share = packet[0, :, part : part + top]

    start = (y * nx + x) * share
    cut = lambda v: lax.dynamic_slice_in_dim(v, start, share, 0)
    sig, total, weight, select = cut(sig), cut(total), cut(weight), cut(select)
    wide = cut(acts).astype(f32)
    g = cut(cotangent).astype(f32)
    sent = weight.astype(bf16).astype(f32)
    score_share = jnp.where(sent > 0.0, score_share / jnp.where(sent > 0.0, sent, 1.0), 0.0)
    dsig = (score_share - jnp.sum(weight * score_share, axis=1, keepdims=True)) / total
    dpick = dsig * sig * (1.0 - sig)
    dlogits = jnp.sum(dpick[:, :, None] * select, axis=1)
    dh_total = dh_share + lax.dot_general(
        dlogits, router.astype(f32), (((1,), (1,)), ((), ())), precision=lax.Precision.HIGHEST
    )
    recip = lax.rsqrt(jnp.mean(wide * wide, axis=-1, keepdims=True) + eps)
    scaled = dh_total * gain
    pulled = recip * scaled - wide * (recip * recip * recip) * jnp.mean(
        wide * scaled, axis=-1, keepdims=True
    )
    return (g + pulled)[None]


def solution(mesh):
    pipe, expert = mesh.devices.shape
    grid = Mesh(
        mesh.devices.reshape(pipe // X, X, expert // CORES, CORES), ("y", "x", "z", "core")
    )
    exp, pipe = ("z", "core"), ("y", "x")
    in_specs = (
        P(exp, None),
        P(exp, None),
        P(),
        P(),
        P(exp, None),
        P(exp, None, pipe),
        P(exp, None, pipe),
        P(exp, pipe, None),
    )
    return jax.shard_map(
        shards, mesh=grid, in_specs=in_specs, out_specs=P(pipe, exp, None), check_vma=False
    )
```

```python
import functools
import jax
import jax.numpy as jnp
from jax import lax
from jax.experimental import pallas as pl
from jax.experimental.pallas import tpu as pltpu
from jax.sharding import Mesh, PartitionSpec as P

eps = 1e-05
X = 4
CORES = 2
LANE = 128
bf16 = jnp.bfloat16
f32 = jnp.float32


def token_weights(acts, gain, router, ids):
    wide = acts.astype(f32)
    recip = lax.rsqrt(jnp.mean(wide * wide, axis=-1, keepdims=True) + eps)
    h = (wide * recip * gain).astype(bf16)
    logits = jnp.dot(h, router, preferred_element_type=f32)
    experts = router.shape[1]
    select = (ids[:, :, None] == jnp.arange(experts, dtype=jnp.int32)[None, None, :]).astype(f32)
    picked = jnp.sum(select * logits[:, None, :], axis=-1)
    sig = jax.nn.sigmoid(picked)
    total = jnp.sum(sig, axis=1, keepdims=True)
    return h, sig, total, sig / total, select


def places(ids, names):
    tokens = ids.shape[0]
    member = jnp.any(ids[:, :, None] == names[None, None, :], axis=1)
    below = (jnp.arange(tokens)[:, None] > jnp.arange(tokens)[None, :]).astype(bf16)
    place = jnp.dot(below, member.astype(bf16), preferred_element_type=f32).astype(jnp.int32)
    return jnp.where(member, place, -4096).T


def at_rows(place, count):
    return place[:, None, :] == jnp.arange(count, dtype=jnp.int32)[None, :, None]


def expert_kernel(cap, nz, rows_hbm, first, second, out_hbm, *scratch):
    h_ref, g_ref, w_ref, out_ref, row_sem, w_sem, out_sem = scratch
    ny, part = rows_hbm.shape[0], rows_hbm.shape[2] // 2
    rank, lane = out_ref.shape[2], out_ref.shape[3]
    pieces = part // lane
    contract = (((1,), (1,)), ((), ()))

    def rows_of(j, ref):
        return [
            pltpu.make_async_copy(
                rows_hbm.at[i, :, pl.ds(j * part, part)],
                ref.at[:, pl.ds(i * part, part)],
                row_sem.at[j, i],
            )
            for i in range(ny)
        ]

    h_copies, g_copies = rows_of(0, h_ref), rows_of(1, g_ref)
    w_copies = [
        [pltpu.make_async_copy(s.at[j], w_ref.at[u, j], w_sem.at[u, j]) for j in range(3)]
        for u, s in enumerate((first, second))
    ]
    def begin(copies):
        for copy in copies:
            copy.start()

    def end(copies):
        for copy in copies:
            copy.wait()

    def times(u, j, ref):
        return lax.dot_general(ref[...], w_ref[u, j], contract, preferred_element_type=f32)

    a, b, dact = [None, None], [None, None], [None, None]
    begin(h_copies + w_copies[0][:1])
    begin(w_copies[0][1:2])
    end(h_copies + w_copies[0][:1])
    begin(g_copies + w_copies[0][2:])
    a[0] = times(0, 0, h_ref)
    end(w_copies[0][1:2])
    begin(w_copies[1][:1])
    b[0] = times(0, 1, h_ref)
    end(g_copies + w_copies[0][2:])
    begin(w_copies[1][1:])
    dact[0] = times(0, 2, g_ref)
    end(w_copies[1][:1])
    a[1] = times(1, 0, h_ref)
    end(w_copies[1][1:])
    b[1] = times(1, 1, h_ref)
    dact[1] = times(1, 2, g_ref)
    score = 0.0
    pulls = []
    for u in range(2):
        sg = jax.nn.sigmoid(a[u])
        sa = a[u] * sg
        act = (sa * b[u]).astype(bf16).astype(f32)
        score = score + jnp.sum(act * dact[u], axis=1, keepdims=True)
        pulls.append((dact[u] * b[u] * sg * (1.0 + a[u] * (1.0 - sg))).astype(bf16))
        pulls.append((dact[u] * sa).astype(bf16))
    lanes = lax.broadcasted_iota(jnp.int32, (cap, lane), 1)
    eye = lanes == lax.broadcasted_iota(jnp.int32, (cap, lane), 0)
    tails = []
    for z in range(nz):
        line = jnp.sum(jnp.where(eye, score[z * cap : (z + 1) * cap], 0.0), axis=0, keepdims=True)
        high = line.astype(bf16).astype(f32)
        tail = [high, line - high]
        if rank > pieces * cap + 2:
            tail.append(jnp.zeros((rank - pieces * cap - 2, lane), f32))
        tails.append(tail)
    stores = []
    for i in range(ny):
        band = pl.ds(i * part, part)
        dh = 0.0
        for u in range(2):
            for j in range(2):
                dh = dh + jnp.dot(pulls[2 * u + j], w_ref[u, j, :, band], preferred_element_type=f32)
        for z in range(nz):
            block = dh[z * cap : (z + 1) * cap]
            block = [block[:, p * lane : (p + 1) * lane] for p in range(pieces)]
            out_ref[i, z] = jnp.concatenate(block + tails[z], axis=0).astype(bf16)
        stores.append(pltpu.make_async_copy(out_ref.at[i], out_hbm.at[i], out_sem.at[i]))
        stores[i].start()
    for copy in stores:
        copy.wait()


def expert_rows(gathered, first, second, nz, cap, rank):
    ny, rows, wide = gathered.shape
    kinds, hidden, width = first.shape
    hbm = pl.BlockSpec(memory_space=pl.ANY)
    return pl.pallas_call(
        functools.partial(expert_kernel, cap, nz),
        out_shape=jax.ShapeDtypeStruct((ny, nz, rank, LANE), bf16),
        in_specs=[hbm] * 3,
        out_specs=hbm,
        scratch_shapes=[
            pltpu.VMEM((rows, width), bf16),
            pltpu.VMEM((rows, width), bf16),
            pltpu.VMEM((2, kinds, hidden, width), bf16),
            pltpu.VMEM((ny, nz, rank, LANE), bf16),
            pltpu.SemaphoreType.DMA((2, ny)),
            pltpu.SemaphoreType.DMA((2, 3)),
            pltpu.SemaphoreType.DMA((ny,)),
        ],
        compiler_params=pltpu.CompilerParams(vmem_limit_bytes=56 * 1024 * 1024),
        cost_estimate=pl.CostEstimate(
            flops=20 * rows * width * hidden,
            bytes_accessed=2 * (3 * rows * width + 6 * width * hidden),
            transcendentals=2 * rows * hidden,
        ),
    )(gathered, first, second)


def shards(acts, cotangent, gain, router, ids, w_gate, w_up, w_down):
    ny, nx, nz, nc = (lax.axis_size(n) for n in ("y", "x", "z", "core"))
    y, x, core = (lax.axis_index(n) for n in ("y", "x", "core"))
    tokens, width = acts.shape
    top = ids.shape[1]
    experts = nz * nc
    cap = min(tokens, (17 * tokens * top + 16 * experts - 1) // (16 * experts))
    part = width // ny
    parity = x % 2

    mine = jnp.stack([w_gate[0].T, w_up[0].T, w_down[0]])
    pairs = []
    for m in range(nx // 2):
        i, j = (2 * m) * nc + 1, (2 * m + 1) * nc
        pairs += [(i, j), (j, i)]
    swapped = lax.ppermute(mine, ("x", "core"), pairs)
    first = jnp.where(core == parity, mine, swapped)
    second = lax.ppermute(first, "core", [(0, 1), (1, 0)])

    h, sig, total, weight, select = token_weights(acts, gain, router, ids)
    names = 2 * jnp.arange(nz, dtype=jnp.int32) + parity
    place = places(ids, names)
    here = at_rows(place, cap)
    of_name = (ids[:, :, None] == names[None, None, :]).astype(f32)
    dense = jnp.sum(of_name * weight[:, :, None], axis=1).astype(bf16)
    h_part = lax.dynamic_slice_in_dim(h, y * part, part, 1)
    g_part = lax.dynamic_slice_in_dim(cotangent, y * part, part, 1)
    rank = -(-cap // 8) * 8
    pick = at_rows(place, rank).astype(bf16)
    scaled = pick * dense.T[:, None, :]
    h_rows = jnp.dot(pick.reshape(nz * rank, tokens), h_part, preferred_element_type=f32)
    dy_rows = jnp.dot(scaled.reshape(nz * rank, tokens), g_part, preferred_element_type=f32)
    rows = jnp.concatenate([h_rows.astype(bf16), dy_rows.astype(bf16)], axis=1)
    rows = lax.all_to_all(rows.reshape(nz, rank, 2 * part), "z", 0, 0, tiled=True)
    rows = rows[:, :cap].reshape(nz * cap, 2 * part)
    gathered = lax.all_gather(rows, "y")

    pieces = part // LANE
    rank = -(-(pieces * cap + 2) // 8) * 8
    back = expert_rows(gathered, first, second, nz, cap, rank)

    back = lax.all_to_all(back.reshape(ny * nz, rank, LANE), ("y", "z"), 0, 0, tiled=True)
    flat = back.reshape(ny * nz * rank, LANE)
    parts = []
    for k in range(pieces):
        spread = at_rows(place + k * cap, rank).astype(bf16)
        spread = jnp.broadcast_to(spread[None], (ny, nz, rank, tokens))
        parts.append(
            lax.dot_general(
                spread.reshape(ny * nz * rank, tokens),
                flat,
                (((0,), (0,)), ((), ())),
                preferred_element_type=f32,
            )
        )
    score = jnp.sum(back[:, pieces * cap : pieces * cap + 2, :cap].astype(f32), axis=1)
    score = score.reshape(ny, nz, cap).sum(axis=0)
    score = jnp.sum(here.astype(f32) * score[:, :, None], axis=1)
    score = jnp.sum(of_name * score.T[:, None, :], axis=-1)
    sections = ny * nx
    share = tokens // sections
    tail = jnp.zeros((tokens, LANE), f32).at[:, :top].set(score)
    packet = jnp.concatenate(parts + [tail], axis=1).reshape(sections, share, part + LANE)
    packet = lax.all_to_all(packet, ("y", "x"), 0, 0, tiled=True)
    packet = packet.reshape(ny, nx, share, part + LANE).sum(axis=1)
    dh_share = jnp.concatenate([packet[i, :, :part] for i in range(ny)], axis=1)
    score_share = packet[0, :, part : part + top]

    start = (y * nx + x) * share
    cut = lambda v: lax.dynamic_slice_in_dim(v, start, share, 0)
    sig, total, weight, select = cut(sig), cut(total), cut(weight), cut(select)
    wide = cut(acts).astype(f32)
    g = cut(cotangent).astype(f32)
    sent = weight.astype(bf16).astype(f32)
    score_share = jnp.where(sent > 0.0, score_share / jnp.where(sent > 0.0, sent, 1.0), 0.0)
    dsig = (score_share - jnp.sum(weight * score_share, axis=1, keepdims=True)) / total
    dpick = dsig * sig * (1.0 - sig)
    dlogits = jnp.sum(dpick[:, :, None] * select, axis=1)
    dh_total = dh_share + lax.dot_general(
        dlogits, router.astype(f32), (((1,), (1,)), ((), ())), precision=lax.Precision.HIGHEST
    )
    recip = lax.rsqrt(jnp.mean(wide * wide, axis=-1, keepdims=True) + eps)
    scaled = dh_total * gain
    pulled = recip * scaled - wide * (recip * recip * recip) * jnp.mean(
        wide * scaled, axis=-1, keepdims=True
    )
    return (g + pulled)[None]


def solution(mesh):
    pipe, expert = mesh.devices.shape
    grid = Mesh(
        mesh.devices.reshape(pipe // X, X, expert // CORES, CORES), ("y", "x", "z", "core")
    )
    exp, pipe = ("z", "core"), ("y", "x")
    in_specs = (
        P(exp, None),
        P(exp, None),
        P(),
        P(),
        P(exp, None),
        P(exp, None, pipe),
        P(exp, None, pipe),
        P(exp, pipe, None),
    )
    return jax.shard_map(
        shards, mesh=grid, in_specs=in_specs, out_specs=P(pipe, exp, None), check_vma=False
    )
```

```python
import functools
import jax
import jax.numpy as jnp
from jax import lax
from jax.experimental import pallas as pl
from jax.experimental.pallas import tpu as pltpu
from jax.sharding import Mesh, PartitionSpec as P

eps = 1e-05
X = 4
CORES = 2
LANE = 128
MAIN = 16
bf16 = jnp.bfloat16
f32 = jnp.float32


def token_weights(acts, gain, router, ids):
    wide = acts.astype(f32)
    recip = lax.rsqrt(jnp.mean(wide * wide, axis=-1, keepdims=True) + eps)
    h = (wide * recip * gain).astype(bf16)
    logits = jnp.dot(h, router, preferred_element_type=f32)
    experts = router.shape[1]
    select = (ids[:, :, None] == jnp.arange(experts, dtype=jnp.int32)[None, None, :]).astype(f32)
    picked = jnp.sum(select * logits[:, None, :], axis=-1)
    sig = jax.nn.sigmoid(picked)
    total = jnp.sum(sig, axis=1, keepdims=True)
    return h, sig, total, sig / total, select


def places(ids, names):
    tokens = ids.shape[0]
    member = jnp.any(ids[:, :, None] == names[None, None, :], axis=1)
    below = (jnp.arange(tokens)[:, None] > jnp.arange(tokens)[None, :]).astype(bf16)
    place = jnp.dot(below, member.astype(bf16), preferred_element_type=f32).astype(jnp.int32)
    return jnp.where(member, place, -4096).T


def at_rows(place, count):
    return place[:, None, :] == jnp.arange(count, dtype=jnp.int32)[None, :, None]


def expert_kernel(nz, info, rows_hbm, others_hbm, *refs):
    mine, (across, left, right, keep_ref, give_ref) = refs[:3], refs[3:8]
    h_ref, g_ref, e_ref, w_ref, row_sem, w_sem = refs[8:]
    ny, rank, lane = keep_ref.shape[0], keep_ref.shape[2], keep_ref.shape[3]
    width = h_ref.shape[2]
    part, fold = width // ny, e_ref.shape[2]
    pieces = part // lane
    count = 2 * nz * MAIN
    contract = (((1,), (1,)), ((), ()))
    own = info[0]
    left, right, across = ([ref.at[j] for j in range(3)] for ref in (left, right, across))

    def fetch(u, j, source):
        return pltpu.make_async_copy(source[j], w_ref.at[u, j], w_sem.at[u, j])

    def start(u, j, if_own, other):
        @pl.when(own == 1)
        def _():
            fetch(u, j, if_own).start()

        @pl.when(own == 0)
        def _():
            fetch(u, j, other).start()

    def begin(copies):
        for copy in copies:
            copy.start()

    def end(copies):
        for copy in copies:
            copy.wait()

    rows = []
    for j, (ref, first, size) in enumerate(
        ((h_ref, 0, width), (g_ref, width, width), (e_ref, 2 * width, fold))
    ):
        rows.append(
            [
                pltpu.make_async_copy(
                    source.at[:, :, pl.ds(first, size)],
                    ref.at[pl.ds(k * nz, nz)],
                    row_sem.at[j, k],
                )
                for k, source in enumerate((rows_hbm, others_hbm))
            ]
        )
    begin(rows[0] + rows[2])
    start(0, 0, mine, left)
    start(0, 1, mine, left)
    end(rows[0] + rows[2])
    begin(rows[1])
    start(0, 2, mine, left)
    half = MAIN // 2
    for i in range(half):
        band = pl.ds(i * fold, fold)
        h_ref[2 * nz, : 2 * nz, band] = e_ref[:, i, :]
    h = h_ref[...].reshape(count + MAIN, width)

    def times(u, j, value):
        return lax.dot_general(value, w_ref[u, j], contract, preferred_element_type=f32)

    a, b, dact = [None, None], [None, None], [None, None]
    fetch(0, 0, mine).wait()
    a[0] = times(0, 0, h)
    fetch(0, 1, mine).wait()
    start(1, 0, across, right)
    start(1, 1, across, right)
    b[0] = times(0, 1, h)
    end(rows[1])
    for i in range(half):
        band = pl.ds(i * fold, fold)
        g_ref[2 * nz, : 2 * nz, band] = e_ref[:, half + i, :]
    g = g_ref[...].reshape(count + MAIN, width)
    fetch(0, 2, mine).wait()
    start(1, 2, across, right)
    dact[0] = times(0, 2, g)
    fetch(1, 0, mine).wait()
    a[1] = times(1, 0, h)
    fetch(1, 1, mine).wait()
    b[1] = times(1, 1, h)
    fetch(1, 2, mine).wait()
    dact[1] = times(1, 2, g)
    score = 0.0
    pulls = []
    for u in range(2):
        sg = jax.nn.sigmoid(a[u])
        sa = a[u] * sg
        act = (sa * b[u]).astype(bf16).astype(f32)
        score = score + jnp.sum(act * dact[u], axis=1, keepdims=True)
        pulls.append((dact[u] * b[u] * sg * (1.0 + a[u] * (1.0 - sg))).astype(bf16))
        pulls.append((dact[u] * sa).astype(bf16))
    lanes = lax.broadcasted_iota(jnp.int32, (MAIN, lane), 1)
    eye = lanes == lax.broadcasted_iota(jnp.int32, (MAIN, lane), 0)
    last = lax.broadcasted_iota(jnp.int32, (1, lane), 1) == MAIN
    gap = jnp.zeros((2, lane), f32)
    over = rank - pieces * (MAIN + 1) - 4
    rest = [jnp.zeros((over, lane), f32)] if over else []
    tails = []
    for n in range(2 * nz):
        line = jnp.where(eye, score[n * MAIN : (n + 1) * MAIN], 0.0)
        line = jnp.sum(line, axis=0, keepdims=True)
        line = line + jnp.where(last, score[count + n : count + n + 1], 0.0)
        high = line.astype(bf16).astype(f32)
        pair = [high, line - high]
        tails.append((pair + [gap] if n < nz else [gap] + pair) + rest)
    for i in range(ny):
        band = pl.ds(i * part, part)
        dh = 0.0
        for u in range(2):
            for j in range(2):
                dh = dh + jnp.dot(pulls[2 * u + j], w_ref[u, j, :, band], preferred_element_type=f32)
        for n in range(2 * nz):
            ref = keep_ref if n < nz else give_ref
            for p in range(pieces):
                cut = slice(p * lane, (p + 1) * lane)
                main = dh[n * MAIN : (n + 1) * MAIN, cut]
                ref[i, n % nz, p * MAIN : (p + 1) * MAIN] = main.astype(ref.dtype)
            end_rows = [
                dh[count + n : count + n + 1, p * lane : (p + 1) * lane] for p in range(pieces)
            ]
            ref[i, n % nz, pieces * MAIN :] = jnp.concatenate(end_rows + tails[n], axis=0).astype(
                ref.dtype
            )


def expert_rows(info, rows, others, slices, ny, rank):
    nz = rows.shape[0]
    kinds, hidden, width = slices[-1].shape
    hbm = pl.BlockSpec(memory_space=pl.ANY)
    vmem = pl.BlockSpec(memory_space=pltpu.VMEM)
    count = (2 * nz + 1) * MAIN
    return pl.pallas_call(
        functools.partial(expert_kernel, nz),
        out_shape=(
            jax.ShapeDtypeStruct((ny, nz, rank, LANE), f32),
            jax.ShapeDtypeStruct((ny, nz, rank, LANE), bf16),
        ),
        in_specs=[pl.BlockSpec(memory_space=pltpu.SMEM)] + [hbm] * 8,
        out_specs=(vmem, vmem),
        scratch_shapes=[
            pltpu.VMEM((2 * nz + 1, MAIN, width), bf16),
            pltpu.VMEM((2 * nz + 1, MAIN, width), bf16),
            pltpu.VMEM((2 * nz, MAIN, 2 * width // MAIN), bf16),
            pltpu.VMEM((2, kinds, hidden, width), bf16),
            pltpu.SemaphoreType.DMA((3, 2)),
            pltpu.SemaphoreType.DMA((2, 3)),
        ],
        compiler_params=pltpu.CompilerParams(vmem_limit_bytes=56 * 1024 * 1024),
        cost_estimate=pl.CostEstimate(
            flops=20 * count * width * hidden,
            bytes_accessed=2 * (4 * count * width + 6 * width * hidden),
            transcendentals=2 * count * hidden,
        ),
    )(info, rows, others, *slices)


def shards(acts, cotangent, gain, router, ids, w_gate, w_up, w_down):
    ny, nx, nz, nc = (lax.axis_size(n) for n in ("y", "x", "z", "core"))
    y, x, core = (lax.axis_index(n) for n in ("y", "x", "core"))
    tokens, width = acts.shape
    top = ids.shape[1]
    experts = nz * nc
    cap = min(tokens, (17 * tokens * top + 16 * experts - 1) // (16 * experts))
    cap = -(-cap // 2)
    assert cap == MAIN + 1 and 2 * nz <= MAIN and ny % 2 == 0
    part = width // ny
    parity = x % 2
    swap = [(0, 1), (1, 0)]

    mine_parts = (w_gate[0].T, w_up[0].T, w_down[0])
    mine = jnp.stack(mine_parts)
    ahead, behind, beside = [], [], []
    for j in range(ny):
        for i in range(nx):
            a = i % 2
            at = lambda yy, xx, cc: (yy * nx + xx % nx) * nc + cc
            ahead.append((at(j, i, 1 - a), at(j, i + 1, a)))
            behind.append((at(j, i, 1 - a), at(j, i - 1, a)))
            beside.append((at(j, i, a), at(j ^ 1, i, a)))
    left = lax.ppermute(mine, ("y", "x", "core"), behind)
    right = lax.ppermute(mine, ("y", "x", "core"), ahead)
    across = lax.ppermute(mine, ("y", "x", "core"), beside)
    info = (core == parity).astype(jnp.int32).reshape(1)

    h, sig, total, weight, select = token_weights(acts, gain, router, ids)
    names = 2 * jnp.arange(nz, dtype=jnp.int32) + parity
    place = places(ids, names)
    halves = [
        jnp.where((place >= n * cap) & (place < (n + 1) * cap), place - n * cap, -4096)
        for n in (0, 1)
    ]
    odd = (x // 2 + y) % 2 == 1
    here = jnp.where(odd, halves[1], halves[0])
    of_name = (ids[:, :, None] == names[None, None, :]).astype(f32)
    dense = jnp.sum(of_name * weight[:, :, None], axis=1).astype(bf16).T

    def picked(scale, values):
        main = (at_rows(here, MAIN).astype(bf16) * scale[:, None, :]).reshape(nz * MAIN, tokens)
        extra = (here == MAIN).astype(bf16) * scale
        main = jnp.dot(main, values, preferred_element_type=f32).astype(bf16)
        extra = jnp.dot(extra, values, preferred_element_type=f32).astype(bf16)
        return main.reshape(nz, MAIN, width), extra.reshape(nz, MAIN // 2, 2 * width // MAIN)

    h_main, h_extra = picked(jnp.ones_like(dense), h)
    dy_main, dy_extra = picked(dense, cotangent)
    extra = jnp.concatenate([h_extra, dy_extra], axis=1)
    rows = jnp.concatenate([h_main, dy_main, extra], axis=2)
    rows = lax.all_to_all(rows, "z", 0, 0, tiled=True)
    others = lax.ppermute(rows, "core", swap)

    pieces = part // LANE
    rank = -(-(pieces * cap + 4) // 8) * 8
    keep, give = expert_rows(info, rows, others, (*mine_parts, across, left, right), ny, rank)
    got = lax.ppermute(give, "core", swap)
    back = (keep + got.astype(f32)).astype(bf16)

    back = lax.all_to_all(back.reshape(ny * nz, rank, LANE), ("y", "z"), 0, 0, tiled=True)
    flat = back.reshape(ny * nz * rank, LANE)
    by_y = [jnp.where(x // 2 % 2 == 1, halves[1 - n], halves[n]) for n in (0, 1)]
    parts = []
    for p in range(pieces):
        spread = []
        for slot in by_y:
            row = jnp.where(slot == MAIN, pieces * MAIN + p, slot + p * MAIN)
            spread.append(at_rows(jnp.where(slot >= 0, row, -1), rank).astype(bf16))
        spread = jnp.broadcast_to(jnp.stack(spread)[None], (ny // 2, 2, nz, rank, tokens))
        parts.append(
            lax.dot_general(
                spread.reshape(ny * nz * rank, tokens),
                flat,
                (((0,), (0,)), ((), ())),
                preferred_element_type=f32,
            )
        )
    score = jnp.sum(back[:, pieces * cap : pieces * cap + 4, :cap].astype(f32), axis=1)
    score = score.reshape(ny // 2, 2, nz, cap).sum(axis=0)
    slots = jnp.stack([at_rows(slot, cap) for slot in by_y]).astype(f32)
    score = jnp.sum(slots * score[:, :, :, None], axis=(0, 2))
    score = jnp.sum(of_name * score.T[:, None, :], axis=-1)
    sections = ny * nx
    share = tokens // sections
    tail = jnp.zeros((tokens, LANE), f32).at[:, :top].set(score)
    packet = jnp.concatenate(parts + [tail], axis=1).reshape(sections, share, part + LANE)
    packet = lax.all_to_all(packet, ("y", "x"), 0, 0, tiled=True)
    packet = packet.reshape(ny, nx, share, part + LANE).sum(axis=1)
    dh_share = jnp.concatenate([packet[i, :, :part] for i in range(ny)], axis=1)
    score_share = packet[0, :, part : part + top]

    start = (y * nx + x) * share
    cut = lambda v: lax.dynamic_slice_in_dim(v, start, share, 0)
    sig, total, weight, select = cut(sig), cut(total), cut(weight), cut(select)
    wide = cut(acts).astype(f32)
    g = cut(cotangent).astype(f32)
    sent = weight.astype(bf16).astype(f32)
    score_share = jnp.where(sent > 0.0, score_share / jnp.where(sent > 0.0, sent, 1.0), 0.0)
    dsig = (score_share - jnp.sum(weight * score_share, axis=1, keepdims=True)) / total
    dpick = dsig * sig * (1.0 - sig)
    dlogits = jnp.sum(dpick[:, :, None] * select, axis=1)
    dh_total = dh_share + lax.dot_general(
        dlogits, router.astype(f32), (((1,), (1,)), ((), ())), precision=lax.Precision.HIGHEST
    )
    recip = lax.rsqrt(jnp.mean(wide * wide, axis=-1, keepdims=True) + eps)
    scaled = dh_total * gain
    pulled = recip * scaled - wide * (recip * recip * recip) * jnp.mean(
        wide * scaled, axis=-1, keepdims=True
    )
    return (g + pulled)[None]


def solution(mesh):
    pipe, expert = mesh.devices.shape
    grid = Mesh(
        mesh.devices.reshape(pipe // X, X, expert // CORES, CORES), ("y", "x", "z", "core")
    )
    exp, pipe = ("z", "core"), ("y", "x")
    in_specs = (
        P(exp, None),
        P(exp, None),
        P(),
        P(),
        P(exp, None),
        P(exp, None, pipe),
        P(exp, None, pipe),
        P(exp, pipe, None),
    )
    return jax.shard_map(
        shards, mesh=grid, in_specs=in_specs, out_specs=P(pipe, exp, None), check_vma=False
    )
```

```python
import functools
import jax
import jax.numpy as jnp
from jax import lax
from jax.experimental import pallas as pl
from jax.experimental.pallas import tpu as pltpu
from jax.sharding import Mesh, PartitionSpec as P

eps = 1e-05
X = 4
CORES = 2
LANE = 128
MAIN = 16
bf16 = jnp.bfloat16
f32 = jnp.float32


def token_weights(acts, gain, router, ids):
    wide = acts.astype(f32)
    recip = lax.rsqrt(jnp.mean(wide * wide, axis=-1, keepdims=True) + eps)
    h = (wide * recip * gain).astype(bf16)
    logits = jnp.dot(h, router, preferred_element_type=f32)
    experts = router.shape[1]
    select = (ids[:, :, None] == jnp.arange(experts, dtype=jnp.int32)[None, None, :]).astype(f32)
    picked = jnp.sum(select * logits[:, None, :], axis=-1)
    sig = jax.nn.sigmoid(picked)
    total = jnp.sum(sig, axis=1, keepdims=True)
    return h, sig, total, sig / total, select


def places(ids, names):
    tokens = ids.shape[0]
    member = jnp.any(ids[:, :, None] == names[None, None, :], axis=1)
    below = (jnp.arange(tokens)[:, None] > jnp.arange(tokens)[None, :]).astype(bf16)
    place = jnp.dot(below, member.astype(bf16), preferred_element_type=f32).astype(jnp.int32)
    return jnp.where(member, place, -4096).T


def at_rows(place, count):
    return place[:, None, :] == jnp.arange(count, dtype=jnp.int32)[None, :, None]


def expert_kernel(nz, info, rows_hbm, others_hbm, *refs):
    mine, (left, other, keep_hbm, give_hbm) = refs[:3], refs[3:7]
    h_ref, g_ref, e_ref, w_ref, keep_ref, give_ref, row_sem, w_sem, out_sem = refs[7:]
    ny, rank, lane = keep_ref.shape[0], keep_ref.shape[2], keep_ref.shape[3]
    width = h_ref.shape[2]
    part, fold = width // ny, e_ref.shape[2]
    pieces = part // lane
    count = 2 * nz * MAIN
    contract = (((1,), (1,)), ((), ()))
    own = info[0]
    left, other = ([ref.at[j] for j in range(3)] for ref in (left, other))

    def fetch(u, j, source):
        return pltpu.make_async_copy(source[j], w_ref.at[u, j], w_sem.at[u, j])

    def start_first(j):
        @pl.when(own == 1)
        def _():
            fetch(0, j, mine).start()

        @pl.when(own == 0)
        def _():
            fetch(0, j, left).start()

    def begin(copies):
        for copy in copies:
            copy.start()

    def end(copies):
        for copy in copies:
            copy.wait()

    rows = []
    for j, (ref, first, size) in enumerate(
        ((h_ref, 0, width), (g_ref, width, width), (e_ref, 2 * width, fold))
    ):
        rows.append(
            [
                pltpu.make_async_copy(
                    source.at[:, :, pl.ds(first, size)],
                    ref.at[pl.ds(k * nz, nz)],
                    row_sem.at[j, k],
                )
                for k, source in enumerate((rows_hbm, others_hbm))
            ]
        )
    begin(rows[0] + rows[2])
    start_first(0)
    start_first(1)
    end(rows[0] + rows[2])
    begin(rows[1])
    start_first(2)
    half = MAIN // 2
    for i in range(half):
        band = pl.ds(i * fold, fold)
        h_ref[2 * nz, : 2 * nz, band] = e_ref[:, i, :]
    h = h_ref[...].reshape(count + MAIN, width)

    def times(u, j, value):
        return lax.dot_general(value, w_ref[u, j], contract, preferred_element_type=f32)

    a, b, dact = [None, None], [None, None], [None, None]
    fetch(0, 0, mine).wait()
    a[0] = times(0, 0, h)
    fetch(0, 1, mine).wait()
    fetch(1, 0, other).start()
    fetch(1, 1, other).start()
    b[0] = times(0, 1, h)
    end(rows[1])
    for i in range(half):
        band = pl.ds(i * fold, fold)
        g_ref[2 * nz, : 2 * nz, band] = e_ref[:, half + i, :]
    g = g_ref[...].reshape(count + MAIN, width)
    fetch(0, 2, mine).wait()
    fetch(1, 2, other).start()
    dact[0] = times(0, 2, g)
    fetch(1, 0, other).wait()
    a[1] = times(1, 0, h)
    fetch(1, 1, other).wait()
    b[1] = times(1, 1, h)
    fetch(1, 2, other).wait()
    dact[1] = times(1, 2, g)
    score = 0.0
    pulls = []
    for u in range(2):
        sg = jax.nn.sigmoid(a[u])
        sa = a[u] * sg
        act = (sa * b[u]).astype(bf16).astype(f32)
        score = score + jnp.sum(act * dact[u], axis=1, keepdims=True)
        pulls.append((dact[u] * b[u] * sg * (1.0 + a[u] * (1.0 - sg))).astype(bf16))
        pulls.append((dact[u] * sa).astype(bf16))
    lanes = lax.broadcasted_iota(jnp.int32, (MAIN, lane), 1)
    eye = lanes == lax.broadcasted_iota(jnp.int32, (MAIN, lane), 0)
    last = lax.broadcasted_iota(jnp.int32, (1, lane), 1) == MAIN
    gap = jnp.zeros((2, lane), f32)
    over = rank - pieces * (MAIN + 1) - 4
    rest = [jnp.zeros((over, lane), f32)] if over else []
    tails = []
    for n in range(2 * nz):
        line = jnp.where(eye, score[n * MAIN : (n + 1) * MAIN], 0.0)
        line = jnp.sum(line, axis=0, keepdims=True)
        line = line + jnp.where(last, score[count + n : count + n + 1], 0.0)
        high = line.astype(bf16).astype(f32)
        pair = [high, line - high]
        tails.append((pair + [gap] if n < nz else [gap] + pair) + rest)
    stores = []
    for i in range(ny):
        band = pl.ds(i * part, part)
        dh = 0.0
        for u in range(2):
            for j in range(2):
                dh = dh + jnp.dot(pulls[2 * u + j], w_ref[u, j, :, band], preferred_element_type=f32)
        for n in range(2 * nz):
            ref = keep_ref if n < nz else give_ref
            for p in range(pieces):
                cut = slice(p * lane, (p + 1) * lane)
                main = dh[n * MAIN : (n + 1) * MAIN, cut]
                ref[i, n % nz, p * MAIN : (p + 1) * MAIN] = main.astype(ref.dtype)
            end_rows = [
                dh[count + n : count + n + 1, p * lane : (p + 1) * lane] for p in range(pieces)
            ]
            ref[i, n % nz, pieces * MAIN :] = jnp.concatenate(end_rows + tails[n], axis=0).astype(
                ref.dtype
            )
        for j, (ref, hbm) in enumerate(((give_ref, give_hbm), (keep_ref, keep_hbm))):
            stores.append(pltpu.make_async_copy(ref.at[i], hbm.at[i], out_sem.at[i, j]))
            stores[-1].start()
    end(stores)


def expert_rows(info, rows, others, slices, ny, rank):
    nz = rows.shape[0]
    kinds, hidden, width = slices[-1].shape
    hbm = pl.BlockSpec(memory_space=pl.ANY)
    count = (2 * nz + 1) * MAIN
    return pl.pallas_call(
        functools.partial(expert_kernel, nz),
        out_shape=(
            jax.ShapeDtypeStruct((ny, nz, rank, LANE), f32),
            jax.ShapeDtypeStruct((ny, nz, rank, LANE), bf16),
        ),
        in_specs=[pl.BlockSpec(memory_space=pltpu.SMEM)] + [hbm] * 7,
        out_specs=(hbm, hbm),
        scratch_shapes=[
            pltpu.VMEM((2 * nz + 1, MAIN, width), bf16),
            pltpu.VMEM((2 * nz + 1, MAIN, width), bf16),
            pltpu.VMEM((2 * nz, MAIN, 2 * width // MAIN), bf16),
            pltpu.VMEM((2, kinds, hidden, width), bf16),
            pltpu.VMEM((ny, nz, rank, LANE), f32),
            pltpu.VMEM((ny, nz, rank, LANE), bf16),
            pltpu.SemaphoreType.DMA((3, 2)),
            pltpu.SemaphoreType.DMA((2, 3)),
            pltpu.SemaphoreType.DMA((ny, 2)),
        ],
        compiler_params=pltpu.CompilerParams(vmem_limit_bytes=52 * 1024 * 1024),
        cost_estimate=pl.CostEstimate(
            flops=20 * count * width * hidden,
            bytes_accessed=2 * (4 * count * width + 6 * width * hidden),
            transcendentals=2 * count * hidden,
        ),
    )(info, rows, others, *slices)


def shards(acts, cotangent, gain, router, ids, w_gate, w_up, w_down):
    ny, nx, nz, nc = (lax.axis_size(n) for n in ("y", "x", "z", "core"))
    y, x, core = (lax.axis_index(n) for n in ("y", "x", "core"))
    tokens, width = acts.shape
    top = ids.shape[1]
    experts = nz * nc
    cap = min(tokens, (17 * tokens * top + 16 * experts - 1) // (16 * experts))
    cap = -(-cap // 2)
    assert cap == MAIN + 1 and 2 * nz <= MAIN and ny % 2 == 0
    part = width // ny
    parity = x % 2
    swap = [(0, 1), (1, 0)]

    mine_parts = (w_gate[0].T, w_up[0].T, w_down[0])
    mine = jnp.stack(mine_parts)
    ahead, behind = [], []
    for j in range(ny):
        for i in range(nx):
            a = i % 2
            at = lambda yy, xx, cc: (yy * nx + xx % nx) * nc + cc
            ahead.append((at(j, i, 1 - a), at(j, i + 1, a)))
            behind.append((at(j, i, 1 - a), at(j, i - 1, a)))
            ahead.append((at(j, i, a), at(j ^ 1, i, a)))
    left = lax.ppermute(mine, ("y", "x", "core"), behind)
    other = lax.ppermute(mine, ("y", "x", "core"), ahead)
    info = (core == parity).astype(jnp.int32).reshape(1)

    h, sig, total, weight, select = token_weights(acts, gain, router, ids)
    names = 2 * jnp.arange(nz, dtype=jnp.int32) + parity
    place = places(ids, names)
    halves = [
        jnp.where((place >= n * cap) & (place < (n + 1) * cap), place - n * cap, -4096)
        for n in (0, 1)
    ]
    odd = (x // 2 + y) % 2 == 1
    here = jnp.where(odd, halves[1], halves[0])
    of_name = (ids[:, :, None] == names[None, None, :]).astype(f32)
    dense = jnp.sum(of_name * weight[:, :, None], axis=1).astype(bf16).T

    def picked(scale, values):
        main = (at_rows(here, MAIN).astype(bf16) * scale[:, None, :]).reshape(nz * MAIN, tokens)
        extra = (here == MAIN).astype(bf16) * scale
        main = jnp.dot(main, values, preferred_element_type=f32).astype(bf16)
        extra = jnp.dot(extra, values, preferred_element_type=f32).astype(bf16)
        return main.reshape(nz, MAIN, width), extra.reshape(nz, MAIN // 2, 2 * width // MAIN)

    h_main, h_extra = picked(jnp.ones_like(dense), h)
    dy_main, dy_extra = picked(dense, cotangent)
    extra = jnp.concatenate([h_extra, dy_extra], axis=1)
    rows = jnp.concatenate([h_main, dy_main, extra], axis=2)
    rows = lax.all_to_all(rows, "z", 0, 0, tiled=True)
    others = lax.ppermute(rows, "core", swap)

    pieces = part // LANE
    rank = -(-(pieces * cap + 4) // 8) * 8
    keep, give = expert_rows(info, rows, others, (*mine_parts, left, other), ny, rank)
    got = lax.ppermute(give, "core", swap)
    back = (keep + got.astype(f32)).astype(bf16)

    back = lax.all_to_all(back.reshape(ny * nz, rank, LANE), ("y", "z"), 0, 0, tiled=True)
    flat = back.reshape(ny * nz * rank, LANE)
    by_y = [jnp.where(x // 2 % 2 == 1, halves[1 - n], halves[n]) for n in (0, 1)]
    parts = []
    for p in range(pieces):
        spread = []
        for slot in by_y:
            row = jnp.where(slot == MAIN, pieces * MAIN + p, slot + p * MAIN)
            spread.append(at_rows(jnp.where(slot >= 0, row, -1), rank).astype(bf16))
        spread = jnp.broadcast_to(jnp.stack(spread)[None], (ny // 2, 2, nz, rank, tokens))
        parts.append(
            lax.dot_general(
                spread.reshape(ny * nz * rank, tokens),
                flat,
                (((0,), (0,)), ((), ())),
                preferred_element_type=f32,
            )
        )
    score = jnp.sum(back[:, pieces * cap : pieces * cap + 4, :cap].astype(f32), axis=1)
    score = score.reshape(ny // 2, 2, nz, cap).sum(axis=0)
    slots = jnp.stack([at_rows(slot, cap) for slot in by_y]).astype(f32)
    score = jnp.sum(slots * score[:, :, :, None], axis=(0, 2))
    score = jnp.sum(of_name * score.T[:, None, :], axis=-1)
    sections = ny * nx
    share = tokens // sections
    high = score.astype(bf16)
    low = (score - high.astype(f32)).astype(bf16)
    tail = jnp.pad(jnp.concatenate([high, low], axis=1), ((0, 0), (0, LANE - 2 * top)))
    packet = [v.astype(bf16).reshape(sections, share, LANE) for v in parts] + [
        tail.reshape(sections, share, LANE)
    ]
    packet = jnp.stack(packet, axis=1).reshape(sections, (pieces + 1) * share, LANE)
    packet = lax.all_to_all(packet, ("y", "x"), 0, 0, tiled=True)
    packet = packet.reshape(ny, nx, pieces + 1, share, LANE).astype(f32).sum(axis=1)
    dh_share = packet[:, :pieces].transpose(2, 0, 1, 3).reshape(share, width)
    score_share = packet[0, pieces, :, :top] + packet[0, pieces, :, top : 2 * top]

    start = (y * nx + x) * share
    cut = lambda v: lax.dynamic_slice_in_dim(v, start, share, 0)
    sig, total, weight, select = cut(sig), cut(total), cut(weight), cut(select)
    wide = cut(acts).astype(f32)
    g = cut(cotangent).astype(f32)
    sent = weight.astype(bf16).astype(f32)
    score_share = jnp.where(sent > 0.0, score_share / jnp.where(sent > 0.0, sent, 1.0), 0.0)
    dsig = (score_share - jnp.sum(weight * score_share, axis=1, keepdims=True)) / total
    dpick = dsig * sig * (1.0 - sig)
    dlogits = jnp.sum(dpick[:, :, None] * select, axis=1)
    dh_total = dh_share + lax.dot_general(
        dlogits, router.astype(f32), (((1,), (1,)), ((), ())), precision=lax.Precision.HIGHEST
    )
    recip = lax.rsqrt(jnp.mean(wide * wide, axis=-1, keepdims=True) + eps)
    scaled = dh_total * gain
    pulled = recip * scaled - wide * (recip * recip * recip) * jnp.mean(
        wide * scaled, axis=-1, keepdims=True
    )
    return (g + pulled)[None]


def solution(mesh):
    pipe, expert = mesh.devices.shape
    grid = Mesh(
        mesh.devices.reshape(pipe // X, X, expert // CORES, CORES), ("y", "x", "z", "core")
    )
    exp, pipe = ("z", "core"), ("y", "x")
    in_specs = (
        P(exp, None),
        P(exp, None),
        P(),
        P(),
        P(exp, None),
        P(exp, None, pipe),
        P(exp, None, pipe),
        P(exp, pipe, None),
    )
    return jax.shard_map(
        shards, mesh=grid, in_specs=in_specs, out_specs=P(pipe, exp, None), check_vma=False
    )
```

```python
import functools
import jax
import jax.numpy as jnp
from jax import lax
from jax.experimental import pallas as pl
from jax.experimental.pallas import tpu as pltpu
from jax.sharding import Mesh, PartitionSpec as P

eps = 1e-05
X = 4
CORES = 2
LANE = 128
MAIN = 16
bf16 = jnp.bfloat16
f32 = jnp.float32


def at_rows(place, count):
    return place[:, None, :] == jnp.arange(count, dtype=jnp.int32)[None, :, None]


def front_kernel(cap, flags, *refs):
    sources, (out, sig_ref, place_ref), copied, sem = refs[:5], refs[5:8], refs[8:13], refs[13]
    copies = [
        pltpu.make_async_copy(source, ref, sem.at[i])
        for i, (source, ref) in enumerate(zip(sources, copied))
    ]
    for copy in copies:
        copy.start()
    for copy in copies:
        copy.wait()
    acts, cotangent, gain, router, ids = copied
    tokens, width = acts.shape
    nz, main, _ = out.shape
    top = ids.shape[0]
    fold = 2 * width // main
    parity, odd = flags[0], flags[1]
    wide = acts[...].astype(f32)
    recip = lax.rsqrt(jnp.mean(wide * wide, axis=1, keepdims=True) + eps)
    h = (wide * recip * gain[...]).astype(bf16)
    logits = lax.dot_general(
        router[...], h, (((1,), (1,)), ((), ())), preferred_element_type=f32
    )
    named = lax.broadcasted_iota(jnp.int32, logits.shape, 0)
    sig = []
    for k in range(top):
        picked = jnp.where(named == ids[k : k + 1], logits, 0.0)
        sig.append(jax.nn.sigmoid(jnp.sum(picked, axis=0, keepdims=True)))
    sig_ref[...] = jnp.concatenate(sig, axis=0)
    total = sum(sig[1:], sig[0])
    names = 2 * lax.broadcasted_iota(jnp.int32, (nz, tokens), 0) + parity
    member = jnp.zeros((nz, tokens), f32)
    dense = jnp.zeros((nz, tokens), f32)
    for k in range(top):
        hit = names == ids[k : k + 1]
        member = jnp.where(hit, 1.0, member)
        dense = jnp.where(hit, sig[k] / total, dense)
    dense = dense.astype(bf16).astype(f32)
    before = lax.broadcasted_iota(jnp.int32, (tokens, tokens), 0)
    before = before < lax.broadcasted_iota(jnp.int32, (tokens, tokens), 1)
    place = jnp.dot(member.astype(bf16), before.astype(bf16), preferred_element_type=f32)
    place = jnp.where(member > 0.0, place.astype(jnp.int32), -4096)
    place_ref[...] = place
    place = place - odd * cap
    slot = lax.broadcasted_iota(jnp.int32, (main, tokens), 0)
    pick, scaled = [], []
    for z in range(nz):
        one = jnp.where(place[z : z + 1] == slot, 1.0, 0.0)
        pick.append(one)
        scaled.append(one * dense[z : z + 1])
    extra = jnp.where(place == main, 1.0, 0.0)
    sides = (
        (h, jnp.concatenate(pick, axis=0), extra),
        (cotangent[...], jnp.concatenate(scaled, axis=0), extra * dense),
    )
    folded = []
    for j, (values, mains, extras) in enumerate(sides):
        rows = jnp.dot(mains.astype(bf16), values, preferred_element_type=f32).astype(bf16)
        for z in range(nz):
            out[z, :, j * width : (j + 1) * width] = rows[z * main : (z + 1) * main]
        folded.append(jnp.dot(extras.astype(bf16), values, preferred_element_type=f32))
    for z in range(nz):
        lines = [v[z : z + 1, i * fold : (i + 1) * fold] for v in folded for i in range(main // 2)]
        out[z, :, 2 * width :] = jnp.concatenate(lines, axis=0).astype(bf16)


def front_rows(flags, acts, cotangent, gain, router, ids, nz, cap):
    tokens, width = acts.shape
    smem, vmem, hbm = (pl.BlockSpec(memory_space=m) for m in (pltpu.SMEM, pltpu.VMEM, pl.ANY))
    values = (acts, cotangent, gain.reshape(1, width), router.T, ids.T)
    return pl.pallas_call(
        functools.partial(front_kernel, cap),
        out_shape=(
            jax.ShapeDtypeStruct((nz, MAIN, 2 * width + 2 * width // MAIN), bf16),
            jax.ShapeDtypeStruct(ids.T.shape, f32),
            jax.ShapeDtypeStruct((nz, tokens), jnp.int32),
        ),
        in_specs=[smem] + [hbm] * 5,
        out_specs=(vmem, vmem, vmem),
        scratch_shapes=[pltpu.VMEM(v.shape, v.dtype) for v in values]
        + [pltpu.SemaphoreType.DMA((5,))],
        compiler_params=pltpu.CompilerParams(vmem_limit_bytes=60 * 1024 * 1024),
        cost_estimate=pl.CostEstimate(
            flops=4 * tokens * tokens * width,
            bytes_accessed=4 * tokens * width + 4 * nz * MAIN * width,
            transcendentals=tokens * 5,
        ),
    )(flags, *values)


def expert_kernel(nz, info, rows_hbm, others_hbm, *refs):
    mine, (left, other, keep_hbm, give_hbm) = refs[:3], refs[3:7]
    h_ref, g_ref, e_ref, w_ref, keep_ref, give_ref, row_sem, w_sem, out_sem = refs[7:]
    ny, rank, lane = keep_ref.shape[0], keep_ref.shape[2], keep_ref.shape[3]
    width = h_ref.shape[2]
    part, fold = width // ny, e_ref.shape[2]
    pieces = part // lane
    count = 2 * nz * MAIN
    contract = (((1,), (1,)), ((), ()))
    own = info[0]
    left, other = ([ref.at[j] for j in range(3)] for ref in (left, other))

    def fetch(u, j, source):
        return pltpu.make_async_copy(source[j], w_ref.at[u, j], w_sem.at[u, j])

    def start_first(j):
        @pl.when(own == 1)
        def _():
            fetch(0, j, mine).start()

        @pl.when(own == 0)
        def _():
            fetch(0, j, left).start()

    def begin(copies):
        for copy in copies:
            copy.start()

    def end(copies):
        for copy in copies:
            copy.wait()

    rows = []
    for j, (ref, first, size) in enumerate(
        ((h_ref, 0, width), (g_ref, width, width), (e_ref, 2 * width, fold))
    ):
        rows.append(
            [
                pltpu.make_async_copy(
                    source.at[:, :, pl.ds(first, size)],
                    ref.at[pl.ds(k * nz, nz)],
                    row_sem.at[j, k],
                )
                for k, source in enumerate((rows_hbm, others_hbm))
            ]
        )
    begin(rows[0] + rows[2])
    start_first(0)
    start_first(1)
    end(rows[0] + rows[2])
    begin(rows[1])
    start_first(2)
    half = MAIN // 2
    for i in range(half):
        band = pl.ds(i * fold, fold)
        h_ref[2 * nz, : 2 * nz, band] = e_ref[:, i, :]
    h = h_ref[...].reshape(count + MAIN, width)

    def times(u, j, value):
        return lax.dot_general(value, w_ref[u, j], contract, preferred_element_type=f32)

    a, b, dact = [None, None], [None, None], [None, None]
    fetch(0, 0, mine).wait()
    a[0] = times(0, 0, h)
    fetch(0, 1, mine).wait()
    fetch(1, 0, other).start()
    fetch(1, 1, other).start()
    b[0] = times(0, 1, h)
    end(rows[1])
    for i in range(half):
        band = pl.ds(i * fold, fold)
        g_ref[2 * nz, : 2 * nz, band] = e_ref[:, half + i, :]
    g = g_ref[...].reshape(count + MAIN, width)
    fetch(0, 2, mine).wait()
    fetch(1, 2, other).start()
    dact[0] = times(0, 2, g)
    fetch(1, 0, other).wait()
    a[1] = times(1, 0, h)
    fetch(1, 1, other).wait()
    b[1] = times(1, 1, h)
    fetch(1, 2, other).wait()
    dact[1] = times(1, 2, g)
    score = 0.0
    pulls = []
    for u in range(2):
        sg = jax.nn.sigmoid(a[u])
        sa = a[u] * sg
        act = (sa * b[u]).astype(bf16).astype(f32)
        score = score + jnp.sum(act * dact[u], axis=1, keepdims=True)
        pulls.append((dact[u] * b[u] * sg * (1.0 + a[u] * (1.0 - sg))).astype(bf16))
        pulls.append((dact[u] * sa).astype(bf16))
    lanes = lax.broadcasted_iota(jnp.int32, (MAIN, lane), 1)
    eye = lanes == lax.broadcasted_iota(jnp.int32, (MAIN, lane), 0)
    last = lax.broadcasted_iota(jnp.int32, (1, lane), 1) == MAIN
    gap = jnp.zeros((2, lane), f32)
    over = rank - pieces * (MAIN + 1) - 4
    rest = [jnp.zeros((over, lane), f32)] if over else []
    tails = []
    for n in range(2 * nz):
        line = jnp.where(eye, score[n * MAIN : (n + 1) * MAIN], 0.0)
        line = jnp.sum(line, axis=0, keepdims=True)
        line = line + jnp.where(last, score[count + n : count + n + 1], 0.0)
        high = line.astype(bf16).astype(f32)
        pair = [high, line - high]
        tails.append((pair + [gap] if n < nz else [gap] + pair) + rest)
    stores = []
    for i in range(ny):
        band = pl.ds(i * part, part)
        dh = 0.0
        for u in range(2):
            for j in range(2):
                dh = dh + jnp.dot(pulls[2 * u + j], w_ref[u, j, :, band], preferred_element_type=f32)
        for n in range(2 * nz):
            ref = keep_ref if n < nz else give_ref
            for p in range(pieces):
                cut = slice(p * lane, (p + 1) * lane)
                main = dh[n * MAIN : (n + 1) * MAIN, cut]
                ref[i, n % nz, p * MAIN : (p + 1) * MAIN] = main.astype(ref.dtype)
            end_rows = [
                dh[count + n : count + n + 1, p * lane : (p + 1) * lane] for p in range(pieces)
            ]
            ref[i, n % nz, pieces * MAIN :] = jnp.concatenate(end_rows + tails[n], axis=0).astype(
                ref.dtype
            )
        for j, (ref, hbm) in enumerate(((give_ref, give_hbm), (keep_ref, keep_hbm))):
            stores.append(pltpu.make_async_copy(ref.at[i], hbm.at[i], out_sem.at[i, j]))
            stores[-1].start()
    end(stores)


def expert_rows(info, rows, others, slices, ny, rank):
    nz = rows.shape[0]
    kinds, hidden, width = slices[-1].shape
    hbm = pl.BlockSpec(memory_space=pl.ANY)
    count = (2 * nz + 1) * MAIN
    return pl.pallas_call(
        functools.partial(expert_kernel, nz),
        out_shape=(
            jax.ShapeDtypeStruct((ny, nz, rank, LANE), bf16),
            jax.ShapeDtypeStruct((ny, nz, rank, LANE), bf16),
        ),
        in_specs=[pl.BlockSpec(memory_space=pltpu.SMEM)] + [hbm] * 7,
        out_specs=(hbm, hbm),
        scratch_shapes=[
            pltpu.VMEM((2 * nz + 1, MAIN, width), bf16),
            pltpu.VMEM((2 * nz + 1, MAIN, width), bf16),
            pltpu.VMEM((2 * nz, MAIN, 2 * width // MAIN), bf16),
            pltpu.VMEM((2, kinds, hidden, width), bf16),
            pltpu.VMEM((ny, nz, rank, LANE), bf16),
            pltpu.VMEM((ny, nz, rank, LANE), bf16),
            pltpu.SemaphoreType.DMA((3, 2)),
            pltpu.SemaphoreType.DMA((2, 3)),
            pltpu.SemaphoreType.DMA((ny, 2)),
        ],
        compiler_params=pltpu.CompilerParams(vmem_limit_bytes=56 * 1024 * 1024),
        cost_estimate=pl.CostEstimate(
            flops=20 * count * width * hidden,
            bytes_accessed=2 * (4 * count * width + 6 * width * hidden),
            transcendentals=2 * count * hidden,
        ),
    )(info, rows, others, *slices)


def shards(acts, cotangent, gain, router, ids, w_gate, w_up, w_down):
    ny, nx, nz, nc = (lax.axis_size(n) for n in ("y", "x", "z", "core"))
    y, x, core = (lax.axis_index(n) for n in ("y", "x", "core"))
    tokens, width = acts.shape
    top = ids.shape[1]
    experts = nz * nc
    cap = min(tokens, (17 * tokens * top + 16 * experts - 1) // (16 * experts))
    cap = -(-cap // 2)
    assert cap == MAIN + 1 and 2 * nz <= MAIN and ny % 2 == 0
    part = width // ny
    parity = x % 2
    swap = [(0, 1), (1, 0)]

    mine_parts = (w_gate[0].T, w_up[0].T, w_down[0])
    mine = jnp.stack(mine_parts)
    ahead, behind = [], []
    for j in range(ny):
        for i in range(nx):
            a = i % 2
            at = lambda yy, xx, cc: (yy * nx + xx % nx) * nc + cc
            ahead.append((at(j, i, 1 - a), at(j, i + 1, a)))
            behind.append((at(j, i, 1 - a), at(j, i - 1, a)))
            ahead.append((at(j, i, a), at(j ^ 1, i, a)))
    left = lax.ppermute(mine, ("y", "x", "core"), behind)
    other = lax.ppermute(mine, ("y", "x", "core"), ahead)
    info = (core == parity).astype(jnp.int32).reshape(1)

    names = 2 * jnp.arange(nz, dtype=jnp.int32) + parity
    flags = jnp.stack([parity, (x // 2 + y) % 2]).astype(jnp.int32)
    rows, sig, place = front_rows(flags, acts, cotangent, gain, router, ids, nz, cap)
    sig = sig.T
    total = jnp.sum(sig, axis=1, keepdims=True)
    weight = sig / total
    select = (ids[:, :, None] == jnp.arange(experts, dtype=jnp.int32)[None, None, :]).astype(f32)
    halves = [
        jnp.where((place >= n * cap) & (place < (n + 1) * cap), place - n * cap, -4096)
        for n in (0, 1)
    ]
    of_name = (ids[:, :, None] == names[None, None, :]).astype(f32)
    rows = lax.all_to_all(rows, "z", 0, 0, tiled=True)
    others = lax.ppermute(rows, "core", swap)

    pieces = part // LANE
    rank = -(-(pieces * cap + 4) // 8) * 8
    keep, give = expert_rows(info, rows, others, (*mine_parts, left, other), ny, rank)
    got = lax.ppermute(give, "core", swap)
    back = (keep.astype(f32) + got.astype(f32)).astype(bf16)

    back = lax.all_to_all(back.reshape(ny * nz, rank, LANE), ("y", "z"), 0, 0, tiled=True)
    flat = back.reshape(ny * nz * rank, LANE)
    by_y = [jnp.where(x // 2 % 2 == 1, halves[1 - n], halves[n]) for n in (0, 1)]
    parts = []
    for p in range(pieces):
        spread = []
        for slot in by_y:
            row = jnp.where(slot == MAIN, pieces * MAIN + p, slot + p * MAIN)
            spread.append(at_rows(jnp.where(slot >= 0, row, -1), rank).astype(bf16))
        spread = jnp.broadcast_to(jnp.stack(spread)[None], (ny // 2, 2, nz, rank, tokens))
        parts.append(
            lax.dot_general(
                spread.reshape(ny * nz * rank, tokens),
                flat,
                (((0,), (0,)), ((), ())),
                preferred_element_type=f32,
            )
        )
    score = jnp.sum(back[:, pieces * cap : pieces * cap + 4, :cap].astype(f32), axis=1)
    score = score.reshape(ny // 2, 2, nz, cap).sum(axis=0)
    slots = jnp.stack([at_rows(slot, cap) for slot in by_y]).astype(f32)
    score = jnp.sum(slots * score[:, :, :, None], axis=(0, 2))
    score = jnp.sum(of_name * score.T[:, None, :], axis=-1)
    sections = ny * nx
    share = tokens // sections
    high = score.astype(bf16)
    low = (score - high.astype(f32)).astype(bf16)
    tail = jnp.pad(jnp.concatenate([high, low], axis=1), ((0, 0), (0, LANE - 2 * top)))
    packet = [v.astype(bf16).reshape(sections, share, LANE) for v in parts] + [
        tail.reshape(sections, share, LANE)
    ]
    packet = jnp.stack(packet, axis=1).reshape(sections, (pieces + 1) * share, LANE)
    packet = lax.all_to_all(packet, ("y", "x"), 0, 0, tiled=True)
    packet = packet.reshape(ny, nx, pieces + 1, share, LANE).astype(f32).sum(axis=1)
    dh_share = packet[:, :pieces].transpose(2, 0, 1, 3).reshape(share, width)
    score_share = packet[0, pieces, :, :top] + packet[0, pieces, :, top : 2 * top]

    start = (y * nx + x) * share
    cut = lambda v: lax.dynamic_slice_in_dim(v, start, share, 0)
    sig, total, weight, select = cut(sig), cut(total), cut(weight), cut(select)
    wide = cut(acts).astype(f32)
    g = cut(cotangent).astype(f32)
    sent = weight.astype(bf16).astype(f32)
    score_share = jnp.where(sent > 0.0, score_share / jnp.where(sent > 0.0, sent, 1.0), 0.0)
    dsig = (score_share - jnp.sum(weight * score_share, axis=1, keepdims=True)) / total
    dpick = dsig * sig * (1.0 - sig)
    dlogits = jnp.sum(dpick[:, :, None] * select, axis=1)
    dh_total = dh_share + lax.dot_general(
        dlogits, router.astype(f32), (((1,), (1,)), ((), ())), precision=lax.Precision.HIGHEST
    )
    recip = lax.rsqrt(jnp.mean(wide * wide, axis=-1, keepdims=True) + eps)
    scaled = dh_total * gain
    pulled = recip * scaled - wide * (recip * recip * recip) * jnp.mean(
        wide * scaled, axis=-1, keepdims=True
    )
    return (g + pulled)[None]


def solution(mesh):
    pipe, expert = mesh.devices.shape
    grid = Mesh(
        mesh.devices.reshape(pipe // X, X, expert // CORES, CORES), ("y", "x", "z", "core")
    )
    exp, pipe = ("z", "core"), ("y", "x")
    in_specs = (
        P(exp, None),
        P(exp, None),
        P(),
        P(),
        P(exp, None),
        P(exp, None, pipe),
        P(exp, None, pipe),
        P(exp, pipe, None),
    )
    return jax.shard_map(
        shards, mesh=grid, in_specs=in_specs, out_specs=P(pipe, exp, None), check_vma=False
    )
```

```python
import functools
import jax
import jax.numpy as jnp
from jax import lax
from jax.experimental import pallas as pl
from jax.experimental.pallas import tpu as pltpu
from jax.sharding import Mesh, PartitionSpec as P

eps = 1e-05
X = 4
CORES = 2
LANE = 128
MAIN = 16
bf16 = jnp.bfloat16
f32 = jnp.float32


def at_rows(place, count):
    return place[:, None, :] == jnp.arange(count, dtype=jnp.int32)[None, :, None]


def front_kernel(cap, *refs):
    sources, weights, (out, sig_ref, place_ref, stacked) = refs[:5], refs[5:8], refs[8:12]
    copied, sem, stack_sem = refs[12:17], refs[17], refs[18]
    copies = [
        pltpu.make_async_copy(source, ref, sem.at[i])
        for i, (source, ref) in enumerate(zip(sources, copied))
    ]
    stacking = [
        pltpu.make_async_copy(weight, stacked.at[j], stack_sem.at[j])
        for j, weight in enumerate(weights)
    ]
    for copy in copies + stacking:
        copy.start()
    for copy in copies:
        copy.wait()
    acts, cotangent, gain, router, ids = copied
    tokens, width = acts.shape
    nz, main, _ = out.shape
    top = ids.shape[0]
    fold = 2 * width // main
    x, y = lax.axis_index("x"), lax.axis_index("y")
    parity, odd = x % 2, (x // 2 + y) % 2
    wide = acts[...].astype(f32)
    recip = lax.rsqrt(jnp.mean(wide * wide, axis=1, keepdims=True) + eps)
    h = (wide * recip * gain[...]).astype(bf16)
    logits = lax.dot_general(
        router[...], h, (((1,), (1,)), ((), ())), preferred_element_type=f32
    )
    named = lax.broadcasted_iota(jnp.int32, logits.shape, 0)
    sig = []
    for k in range(top):
        picked = jnp.where(named == ids[k : k + 1], logits, 0.0)
        sig.append(jax.nn.sigmoid(jnp.sum(picked, axis=0, keepdims=True)))
    sig_ref[...] = jnp.concatenate(sig, axis=0)
    total = sum(sig[1:], sig[0])
    names = 2 * lax.broadcasted_iota(jnp.int32, (nz, tokens), 0) + parity
    member = jnp.zeros((nz, tokens), f32)
    dense = jnp.zeros((nz, tokens), f32)
    for k in range(top):
        hit = names == ids[k : k + 1]
        member = jnp.where(hit, 1.0, member)
        dense = jnp.where(hit, sig[k] / total, dense)
    dense = dense.astype(bf16).astype(f32)
    before = lax.broadcasted_iota(jnp.int32, (tokens, tokens), 0)
    before = before < lax.broadcasted_iota(jnp.int32, (tokens, tokens), 1)
    place = jnp.dot(member.astype(bf16), before.astype(bf16), preferred_element_type=f32)
    place = jnp.where(member > 0.0, place.astype(jnp.int32), -4096)
    place_ref[...] = place
    place = place - odd * cap
    slot = lax.broadcasted_iota(jnp.int32, (main, tokens), 0)
    pick, scaled = [], []
    for z in range(nz):
        one = jnp.where(place[z : z + 1] == slot, 1.0, 0.0)
        pick.append(one)
        scaled.append(one * dense[z : z + 1])
    extra = jnp.where(place == main, 1.0, 0.0)
    sides = (
        (h, jnp.concatenate(pick, axis=0), extra),
        (cotangent[...], jnp.concatenate(scaled, axis=0), extra * dense),
    )
    folded = []
    for j, (values, mains, extras) in enumerate(sides):
        rows = jnp.dot(mains.astype(bf16), values, preferred_element_type=f32).astype(bf16)
        for z in range(nz):
            out[z, :, j * width : (j + 1) * width] = rows[z * main : (z + 1) * main]
        folded.append(jnp.dot(extras.astype(bf16), values, preferred_element_type=f32))
    for z in range(nz):
        lines = [v[z : z + 1, i * fold : (i + 1) * fold] for v in folded for i in range(main // 2)]
        out[z, :, 2 * width :] = jnp.concatenate(lines, axis=0).astype(bf16)
    for copy in stacking:
        copy.wait()


def front_rows(acts, cotangent, gain, router, ids, weights, nz, cap):
    tokens, width = acts.shape
    vmem, hbm = (pl.BlockSpec(memory_space=m) for m in (pltpu.VMEM, pl.ANY))
    values = (acts, cotangent, gain.reshape(1, width), router.T, ids.T)
    return pl.pallas_call(
        functools.partial(front_kernel, cap),
        out_shape=(
            jax.ShapeDtypeStruct((nz, MAIN, 2 * width + 2 * width // MAIN), bf16),
            jax.ShapeDtypeStruct(ids.T.shape, f32),
            jax.ShapeDtypeStruct((nz, tokens), jnp.int32),
            jax.ShapeDtypeStruct((3, *weights[0].shape), bf16),
        ),
        in_specs=[hbm] * 8,
        out_specs=(vmem, vmem, vmem, hbm),
        scratch_shapes=[pltpu.VMEM(v.shape, v.dtype) for v in values]
        + [pltpu.SemaphoreType.DMA((5,)), pltpu.SemaphoreType.DMA((3,))],
        compiler_params=pltpu.CompilerParams(vmem_limit_bytes=60 * 1024 * 1024),
        cost_estimate=pl.CostEstimate(
            flops=4 * tokens * tokens * width,
            bytes_accessed=4 * tokens * width + 4 * nz * MAIN * width,
            transcendentals=tokens * 5,
        ),
    )(*values, *weights)


def expert_kernel(nz, rows_hbm, others_hbm, *refs):
    mine, left, other, keep_hbm, give_hbm = refs[:5]
    h_ref, g_ref, e_ref, w_ref, keep_ref, give_ref, row_sem, w_sem, out_sem = refs[5:]
    ny, rank, lane = keep_ref.shape[0], keep_ref.shape[2], keep_ref.shape[3]
    width = h_ref.shape[2]
    part, fold = width // ny, e_ref.shape[2]
    pieces = part // lane
    count = 2 * nz * MAIN
    contract = (((1,), (1,)), ((), ()))
    own = (lax.axis_index("core") == lax.axis_index("x") % 2).astype(jnp.int32)

    def fetch(u, j, source):
        return pltpu.make_async_copy(source.at[j], w_ref.at[u, j], w_sem.at[u, j])

    def start_first(j):
        @pl.when(own == 1)
        def _():
            fetch(0, j, mine).start()

        @pl.when(own == 0)
        def _():
            fetch(0, j, left).start()

    def begin(copies):
        for copy in copies:
            copy.start()

    def end(copies):
        for copy in copies:
            copy.wait()

    rows = []
    for j, (ref, first, size) in enumerate(
        ((h_ref, 0, width), (g_ref, width, width), (e_ref, 2 * width, fold))
    ):
        rows.append(
            [
                pltpu.make_async_copy(
                    source.at[:, :, pl.ds(first, size)],
                    ref.at[pl.ds(k * nz, nz)],
                    row_sem.at[j, k],
                )
                for k, source in enumerate((rows_hbm, others_hbm))
            ]
        )
    begin(rows[0] + rows[2])
    start_first(0)
    start_first(1)
    end(rows[0] + rows[2])
    begin(rows[1])
    start_first(2)
    half = MAIN // 2
    for i in range(half):
        band = pl.ds(i * fold, fold)
        h_ref[2 * nz, : 2 * nz, band] = e_ref[:, i, :]
    h = h_ref[...].reshape(count + MAIN, width)

    def times(u, j, value):
        return lax.dot_general(value, w_ref[u, j], contract, preferred_element_type=f32)

    a, b, dact = [None, None], [None, None], [None, None]
    fetch(0, 0, mine).wait()
    a[0] = times(0, 0, h)
    fetch(0, 1, mine).wait()
    fetch(1, 0, other).start()
    fetch(1, 1, other).start()
    b[0] = times(0, 1, h)
    end(rows[1])
    for i in range(half):
        band = pl.ds(i * fold, fold)
        g_ref[2 * nz, : 2 * nz, band] = e_ref[:, half + i, :]
    g = g_ref[...].reshape(count + MAIN, width)
    fetch(0, 2, mine).wait()
    fetch(1, 2, other).start()
    dact[0] = times(0, 2, g)
    fetch(1, 0, other).wait()
    a[1] = times(1, 0, h)
    fetch(1, 1, other).wait()
    b[1] = times(1, 1, h)
    fetch(1, 2, other).wait()
    dact[1] = times(1, 2, g)
    score = 0.0
    pulls = []
    for u in range(2):
        sg = jax.nn.sigmoid(a[u])
        sa = a[u] * sg
        act = (sa * b[u]).astype(bf16).astype(f32)
        score = score + jnp.sum(act * dact[u], axis=1, keepdims=True)
        pulls.append((dact[u] * b[u] * sg * (1.0 + a[u] * (1.0 - sg))).astype(bf16))
        pulls.append((dact[u] * sa).astype(bf16))
    lanes = lax.broadcasted_iota(jnp.int32, (MAIN, lane), 1)
    eye = lanes == lax.broadcasted_iota(jnp.int32, (MAIN, lane), 0)
    last = lax.broadcasted_iota(jnp.int32, (1, lane), 1) == MAIN
    gap = jnp.zeros((2, lane), f32)
    over = rank - pieces * (MAIN + 1) - 4
    rest = [jnp.zeros((over, lane), f32)] if over else []
    tails = []
    for n in range(2 * nz):
        line = jnp.where(eye, score[n * MAIN : (n + 1) * MAIN], 0.0)
        line = jnp.sum(line, axis=0, keepdims=True)
        line = line + jnp.where(last, score[count + n : count + n + 1], 0.0)
        high = line.astype(bf16).astype(f32)
        pair = [high, line - high]
        tails.append((pair + [gap] if n < nz else [gap] + pair) + rest)
    stores = []
    for i in range(ny):
        band = pl.ds(i * part, part)
        dh = 0.0
        for u in range(2):
            for j in range(2):
                dh = dh + jnp.dot(pulls[2 * u + j], w_ref[u, j, :, band], preferred_element_type=f32)
        for n in range(2 * nz):
            ref = keep_ref if n < nz else give_ref
            for p in range(pieces):
                cut = slice(p * lane, (p + 1) * lane)
                main = dh[n * MAIN : (n + 1) * MAIN, cut]
                ref[i, n % nz, p * MAIN : (p + 1) * MAIN] = main.astype(ref.dtype)
            end_rows = [
                dh[count + n : count + n + 1, p * lane : (p + 1) * lane] for p in range(pieces)
            ]
            ref[i, n % nz, pieces * MAIN :] = jnp.concatenate(end_rows + tails[n], axis=0).astype(
                ref.dtype
            )
        for j, (ref, hbm) in enumerate(((give_ref, give_hbm), (keep_ref, keep_hbm))):
            stores.append(pltpu.make_async_copy(ref.at[i], hbm.at[i], out_sem.at[i, j]))
            stores[-1].start()
    end(stores)


def expert_rows(rows, others, slices, ny, rank):
    nz = rows.shape[0]
    kinds, hidden, width = slices[0].shape
    hbm = pl.BlockSpec(memory_space=pl.ANY)
    count = (2 * nz + 1) * MAIN
    return pl.pallas_call(
        functools.partial(expert_kernel, nz),
        out_shape=(
            jax.ShapeDtypeStruct((ny, nz, rank, LANE), bf16),
            jax.ShapeDtypeStruct((ny, nz, rank, LANE), bf16),
        ),
        in_specs=[hbm] * 5,
        out_specs=(hbm, hbm),
        scratch_shapes=[
            pltpu.VMEM((2 * nz + 1, MAIN, width), bf16),
            pltpu.VMEM((2 * nz + 1, MAIN, width), bf16),
            pltpu.VMEM((2 * nz, MAIN, 2 * width // MAIN), bf16),
            pltpu.VMEM((2, kinds, hidden, width), bf16),
            pltpu.VMEM((ny, nz, rank, LANE), bf16),
            pltpu.VMEM((ny, nz, rank, LANE), bf16),
            pltpu.SemaphoreType.DMA((3, 2)),
            pltpu.SemaphoreType.DMA((2, 3)),
            pltpu.SemaphoreType.DMA((ny, 2)),
        ],
        compiler_params=pltpu.CompilerParams(vmem_limit_bytes=48 * 1024 * 1024),
        cost_estimate=pl.CostEstimate(
            flops=20 * count * width * hidden,
            bytes_accessed=2 * (4 * count * width + 6 * width * hidden),
            transcendentals=2 * count * hidden,
        ),
    )(rows, others, *slices)


def shards(acts, cotangent, gain, router, ids, w_gate, w_up, w_down):
    ny, nx, nz, nc = (lax.axis_size(n) for n in ("y", "x", "z", "core"))
    y, x, core = (lax.axis_index(n) for n in ("y", "x", "core"))
    tokens, width = acts.shape
    top = ids.shape[1]
    experts = nz * nc
    cap = min(tokens, (17 * tokens * top + 16 * experts - 1) // (16 * experts))
    cap = -(-cap // 2)
    assert cap == MAIN + 1 and 2 * nz <= MAIN and ny % 2 == 0
    part = width // ny
    parity = x % 2
    swap = [(0, 1), (1, 0)]

    ahead, behind = [], []
    for j in range(ny):
        for i in range(nx):
            a = i % 2
            at = lambda yy, xx, cc: (yy * nx + xx % nx) * nc + cc
            ahead.append((at(j, i, 1 - a), at(j, i + 1, a)))
            behind.append((at(j, i, 1 - a), at(j, i - 1, a)))
            ahead.append((at(j, i, a), at(j ^ 1, i, a)))

    names = 2 * jnp.arange(nz, dtype=jnp.int32) + parity
    weights = (w_gate[0].T, w_up[0].T, w_down[0])
    rows, sig, place, mine = front_rows(acts, cotangent, gain, router, ids, weights, nz, cap)
    left = lax.ppermute(mine, ("y", "x", "core"), behind)
    other = lax.ppermute(mine, ("y", "x", "core"), ahead)
    sig = sig.T
    total = jnp.sum(sig, axis=1, keepdims=True)
    weight = sig / total
    select = (ids[:, :, None] == jnp.arange(experts, dtype=jnp.int32)[None, None, :]).astype(f32)
    halves = [
        jnp.where((place >= n * cap) & (place < (n + 1) * cap), place - n * cap, -4096)
        for n in (0, 1)
    ]
    of_name = (ids[:, :, None] == names[None, None, :]).astype(f32)
    rows = lax.all_to_all(rows, "z", 0, 0, tiled=True)
    others = lax.ppermute(rows, "core", swap)

    pieces = part // LANE
    rank = -(-(pieces * cap + 4) // 8) * 8
    keep, give = expert_rows(rows, others, (mine, left, other), ny, rank)
    got = lax.ppermute(give, "core", swap)
    back = (keep.astype(f32) + got.astype(f32)).astype(bf16)

    back = lax.all_to_all(back.reshape(ny * nz, rank, LANE), ("y", "z"), 0, 0, tiled=True)
    flat = back.reshape(ny * nz * rank, LANE)
    by_y = [jnp.where(x // 2 % 2 == 1, halves[1 - n], halves[n]) for n in (0, 1)]
    parts = []
    for p in range(pieces):
        spread = []
        for slot in by_y:
            row = jnp.where(slot == MAIN, pieces * MAIN + p, slot + p * MAIN)
            spread.append(at_rows(jnp.where(slot >= 0, row, -1), rank).astype(bf16))
        spread = jnp.broadcast_to(jnp.stack(spread)[None], (ny // 2, 2, nz, rank, tokens))
        parts.append(
            lax.dot_general(
                spread.reshape(ny * nz * rank, tokens),
                flat,
                (((0,), (0,)), ((), ())),
                preferred_element_type=f32,
            )
        )
    score = jnp.sum(back[:, pieces * cap : pieces * cap + 4, :cap].astype(f32), axis=1)
    score = score.reshape(ny // 2, 2, nz, cap).sum(axis=0)
    slots = jnp.stack([at_rows(slot, cap) for slot in by_y]).astype(f32)
    score = jnp.sum(slots * score[:, :, :, None], axis=(0, 2))
    score = jnp.sum(of_name * score.T[:, None, :], axis=-1)
    sections = ny * nx
    share = tokens // sections
    high = score.astype(bf16)
    low = (score - high.astype(f32)).astype(bf16)
    tail = jnp.pad(jnp.concatenate([high, low], axis=1), ((0, 0), (0, LANE - 2 * top)))
    packet = [v.astype(bf16).reshape(sections, share, LANE) for v in parts] + [
        tail.reshape(sections, share, LANE)
    ]
    packet = jnp.stack(packet, axis=1).reshape(sections, (pieces + 1) * share, LANE)
    packet = lax.all_to_all(packet, ("y", "x"), 0, 0, tiled=True)
    packet = packet.reshape(ny, nx, pieces + 1, share, LANE).astype(f32).sum(axis=1)
    dh_share = packet[:, :pieces].transpose(2, 0, 1, 3).reshape(share, width)
    score_share = packet[0, pieces, :, :top] + packet[0, pieces, :, top : 2 * top]

    start = (y * nx + x) * share
    cut = lambda v: lax.dynamic_slice_in_dim(v, start, share, 0)
    sig, total, weight, select = cut(sig), cut(total), cut(weight), cut(select)
    wide = cut(acts).astype(f32)
    g = cut(cotangent).astype(f32)
    sent = weight.astype(bf16).astype(f32)
    score_share = jnp.where(sent > 0.0, score_share / jnp.where(sent > 0.0, sent, 1.0), 0.0)
    dsig = (score_share - jnp.sum(weight * score_share, axis=1, keepdims=True)) / total
    dpick = dsig * sig * (1.0 - sig)
    dlogits = jnp.sum(dpick[:, :, None] * select, axis=1)
    dh_total = dh_share + lax.dot_general(
        dlogits, router.astype(f32), (((1,), (1,)), ((), ())), precision=lax.Precision.HIGHEST
    )
    recip = lax.rsqrt(jnp.mean(wide * wide, axis=-1, keepdims=True) + eps)
    scaled = dh_total * gain
    pulled = recip * scaled - wide * (recip * recip * recip) * jnp.mean(
        wide * scaled, axis=-1, keepdims=True
    )
    return (g + pulled)[None]


def solution(mesh):
    pipe, expert = mesh.devices.shape
    grid = Mesh(
        mesh.devices.reshape(pipe // X, X, expert // CORES, CORES), ("y", "x", "z", "core")
    )
    exp, pipe = ("z", "core"), ("y", "x")
    in_specs = (
        P(exp, None),
        P(exp, None),
        P(),
        P(),
        P(exp, None),
        P(exp, None, pipe),
        P(exp, None, pipe),
        P(exp, pipe, None),
    )
    return jax.shard_map(
        shards, mesh=grid, in_specs=in_specs, out_specs=P(pipe, exp, None), check_vma=False
    )
```

```python
import functools
import jax
import jax.numpy as jnp
from jax import lax
from jax.experimental import pallas as pl
from jax.experimental.pallas import tpu as pltpu
from jax.sharding import Mesh, PartitionSpec as P

eps = 1e-05
X = 4
CORES = 2
LANE = 128
MAIN = 16
bf16 = jnp.bfloat16
f32 = jnp.float32


def at_rows(place, count):
    return place[:, None, :] == jnp.arange(count, dtype=jnp.int32)[None, :, None]


def front_kernel(cap, *refs):
    sources, (out, sig_ref, place_ref), copied, sem = refs[:5], refs[5:8], refs[8:13], refs[13]
    copies = [
        pltpu.make_async_copy(source, ref, sem.at[i])
        for i, (source, ref) in enumerate(zip(sources, copied))
    ]
    for copy in copies:
        copy.start()
    for copy in copies:
        copy.wait()
    acts, cotangent, gain, router, ids = copied
    tokens, width = acts.shape
    nz, main, _ = out.shape
    top = ids.shape[0]
    fold = 2 * width // main
    x, y = lax.axis_index("x"), lax.axis_index("y")
    parity, odd = x % 2, (x // 2 + y) % 2
    wide = acts[...].astype(f32)
    recip = lax.rsqrt(jnp.mean(wide * wide, axis=1, keepdims=True) + eps)
    h = (wide * recip * gain[...]).astype(bf16)
    logits = lax.dot_general(
        router[...], h, (((1,), (1,)), ((), ())), preferred_element_type=f32
    )
    named = lax.broadcasted_iota(jnp.int32, logits.shape, 0)
    sig = []
    for k in range(top):
        picked = jnp.where(named == ids[k : k + 1], logits, 0.0)
        sig.append(jax.nn.sigmoid(jnp.sum(picked, axis=0, keepdims=True)))
    sig_ref[...] = jnp.concatenate(sig, axis=0)
    total = sum(sig[1:], sig[0])
    names = 2 * lax.broadcasted_iota(jnp.int32, (nz, tokens), 0) + parity
    member = jnp.zeros((nz, tokens), f32)
    dense = jnp.zeros((nz, tokens), f32)
    for k in range(top):
        hit = names == ids[k : k + 1]
        member = jnp.where(hit, 1.0, member)
        dense = jnp.where(hit, sig[k] / total, dense)
    dense = dense.astype(bf16).astype(f32)
    before = lax.broadcasted_iota(jnp.int32, (tokens, tokens), 0)
    before = before < lax.broadcasted_iota(jnp.int32, (tokens, tokens), 1)
    place = jnp.dot(member.astype(bf16), before.astype(bf16), preferred_element_type=f32)
    place = jnp.where(member > 0.0, place.astype(jnp.int32), -4096)
    place_ref[...] = place
    place = place - odd * cap
    slot = lax.broadcasted_iota(jnp.int32, (main, tokens), 0)
    pick, scaled = [], []
    for z in range(nz):
        one = jnp.where(place[z : z + 1] == slot, 1.0, 0.0)
        pick.append(one)
        scaled.append(one * dense[z : z + 1])
    extra = jnp.where(place == main, 1.0, 0.0)
    sides = (
        (h, jnp.concatenate(pick, axis=0), extra),
        (cotangent[...], jnp.concatenate(scaled, axis=0), extra * dense),
    )
    folded = []
    for j, (values, mains, extras) in enumerate(sides):
        rows = jnp.dot(mains.astype(bf16), values, preferred_element_type=f32).astype(bf16)
        for z in range(nz):
            out[z, :, j * width : (j + 1) * width] = rows[z * main : (z + 1) * main]
        folded.append(jnp.dot(extras.astype(bf16), values, preferred_element_type=f32))
    for z in range(nz):
        lines = [v[z : z + 1, i * fold : (i + 1) * fold] for v in folded for i in range(main // 2)]
        out[z, :, 2 * width :] = jnp.concatenate(lines, axis=0).astype(bf16)


def front_rows(acts, cotangent, gain, router, ids, nz, cap):
    tokens, width = acts.shape
    vmem, hbm = (pl.BlockSpec(memory_space=m) for m in (pltpu.VMEM, pl.ANY))
    values = (acts, cotangent, gain.reshape(1, width), router.T, ids.T)
    return pl.pallas_call(
        functools.partial(front_kernel, cap),
        out_shape=(
            jax.ShapeDtypeStruct((nz, MAIN, 2 * width + 2 * width // MAIN), bf16),
            jax.ShapeDtypeStruct(ids.T.shape, f32),
            jax.ShapeDtypeStruct((nz, tokens), jnp.int32),
        ),
        in_specs=[hbm] * 5,
        out_specs=(vmem, vmem, vmem),
        scratch_shapes=[pltpu.VMEM(v.shape, v.dtype) for v in values]
        + [pltpu.SemaphoreType.DMA((5,))],
        compiler_params=pltpu.CompilerParams(vmem_limit_bytes=60 * 1024 * 1024),
        cost_estimate=pl.CostEstimate(
            flops=4 * tokens * tokens * width,
            bytes_accessed=4 * tokens * width + 4 * nz * MAIN * width,
            transcendentals=tokens * 5,
        ),
    )(*values)


def expert_kernel(nz, rows_hbm, others_hbm, *refs):
    mine, left, other, keep_hbm, give_hbm = refs[:5]
    h_ref, g_ref, e_ref, w_ref, keep_ref, give_ref, row_sem, w_sem, out_sem = refs[5:]
    ny, rank, lane = keep_ref.shape[0], keep_ref.shape[2], keep_ref.shape[3]
    width = h_ref.shape[2]
    part, fold = width // ny, e_ref.shape[2]
    pieces = part // lane
    count = 2 * nz * MAIN
    contract = (((1,), (1,)), ((), ()))
    own = (lax.axis_index("core") == lax.axis_index("x") % 2).astype(jnp.int32)

    def fetch(u, j, source):
        return pltpu.make_async_copy(source.at[j], w_ref.at[u, j], w_sem.at[u, j])

    def start_first(j):
        @pl.when(own == 1)
        def _():
            fetch(0, j, mine).start()

        @pl.when(own == 0)
        def _():
            fetch(0, j, left).start()

    def begin(copies):
        for copy in copies:
            copy.start()

    def end(copies):
        for copy in copies:
            copy.wait()

    rows = []
    for j, (ref, first, size) in enumerate(
        ((h_ref, 0, width), (g_ref, width, width), (e_ref, 2 * width, fold))
    ):
        rows.append(
            [
                pltpu.make_async_copy(
                    source.at[:, :, pl.ds(first, size)],
                    ref.at[pl.ds(k * nz, nz)],
                    row_sem.at[j, k],
                )
                for k, source in enumerate((rows_hbm, others_hbm))
            ]
        )
    begin(rows[0] + rows[2])
    start_first(0)
    start_first(1)
    end(rows[0] + rows[2])
    begin(rows[1])
    start_first(2)
    half = MAIN // 2
    for i in range(half):
        band = pl.ds(i * fold, fold)
        h_ref[2 * nz, : 2 * nz, band] = e_ref[:, i, :]
    h = h_ref[...].reshape(count + MAIN, width)

    def times(u, j, value):
        return lax.dot_general(value, w_ref[u, j], contract, preferred_element_type=f32)

    a, b, dact = [None, None], [None, None], [None, None]
    fetch(0, 0, mine).wait()
    a[0] = times(0, 0, h)
    fetch(0, 1, mine).wait()
    fetch(1, 0, other).start()
    fetch(1, 1, other).start()
    b[0] = times(0, 1, h)
    end(rows[1])
    for i in range(half):
        band = pl.ds(i * fold, fold)
        g_ref[2 * nz, : 2 * nz, band] = e_ref[:, half + i, :]
    g = g_ref[...].reshape(count + MAIN, width)
    fetch(0, 2, mine).wait()
    fetch(1, 2, other).start()
    dact[0] = times(0, 2, g)
    fetch(1, 0, other).wait()
    a[1] = times(1, 0, h)
    fetch(1, 1, other).wait()
    b[1] = times(1, 1, h)
    fetch(1, 2, other).wait()
    dact[1] = times(1, 2, g)
    score = 0.0
    pulls = []
    for u in range(2):
        sg = jax.nn.sigmoid(a[u])
        sa = a[u] * sg
        act = (sa * b[u]).astype(bf16).astype(f32)
        score = score + jnp.sum(act * dact[u], axis=1, keepdims=True)
        pulls.append((dact[u] * b[u] * sg * (1.0 + a[u] * (1.0 - sg))).astype(bf16))
        pulls.append((dact[u] * sa).astype(bf16))
    lanes = lax.broadcasted_iota(jnp.int32, (MAIN, lane), 1)
    eye = lanes == lax.broadcasted_iota(jnp.int32, (MAIN, lane), 0)
    last = lax.broadcasted_iota(jnp.int32, (1, lane), 1) == MAIN
    gap = jnp.zeros((2, lane), f32)
    over = rank - pieces * (MAIN + 1) - 4
    rest = [jnp.zeros((over, lane), f32)] if over else []
    tails = []
    for n in range(2 * nz):
        line = jnp.where(eye, score[n * MAIN : (n + 1) * MAIN], 0.0)
        line = jnp.sum(line, axis=0, keepdims=True)
        line = line + jnp.where(last, score[count + n : count + n + 1], 0.0)
        high = line.astype(bf16).astype(f32)
        pair = [high, line - high]
        tails.append((pair + [gap] if n < nz else [gap] + pair) + rest)
    stores = []
    for i in range(ny):
        band = pl.ds(i * part, part)
        dh = 0.0
        for u in range(2):
            for j in range(2):
                dh = dh + jnp.dot(pulls[2 * u + j], w_ref[u, j, :, band], preferred_element_type=f32)
        for n in range(2 * nz):
            ref = keep_ref if n < nz else give_ref
            for p in range(pieces):
                cut = slice(p * lane, (p + 1) * lane)
                main = dh[n * MAIN : (n + 1) * MAIN, cut]
                ref[i, n % nz, p * MAIN : (p + 1) * MAIN] = main.astype(ref.dtype)
            end_rows = [
                dh[count + n : count + n + 1, p * lane : (p + 1) * lane] for p in range(pieces)
            ]
            ref[i, n % nz, pieces * MAIN :] = jnp.concatenate(end_rows + tails[n], axis=0).astype(
                ref.dtype
            )
        for j, (ref, hbm) in enumerate(((give_ref, give_hbm), (keep_ref, keep_hbm))):
            stores.append(pltpu.make_async_copy(ref.at[i], hbm.at[i], out_sem.at[i, j]))
            stores[-1].start()
    end(stores)


def expert_rows(rows, others, slices, ny, rank):
    nz = rows.shape[0]
    kinds, hidden, width = slices[0].shape
    hbm = pl.BlockSpec(memory_space=pl.ANY)
    count = (2 * nz + 1) * MAIN
    return pl.pallas_call(
        functools.partial(expert_kernel, nz),
        out_shape=(
            jax.ShapeDtypeStruct((ny, nz, rank, LANE), bf16),
            jax.ShapeDtypeStruct((ny, nz, rank, LANE), bf16),
        ),
        in_specs=[hbm] * 5,
        out_specs=(hbm, hbm),
        scratch_shapes=[
            pltpu.VMEM((2 * nz + 1, MAIN, width), bf16),
            pltpu.VMEM((2 * nz + 1, MAIN, width), bf16),
            pltpu.VMEM((2 * nz, MAIN, 2 * width // MAIN), bf16),
            pltpu.VMEM((2, kinds, hidden, width), bf16),
            pltpu.VMEM((ny, nz, rank, LANE), bf16),
            pltpu.VMEM((ny, nz, rank, LANE), bf16),
            pltpu.SemaphoreType.DMA((3, 2)),
            pltpu.SemaphoreType.DMA((2, 3)),
            pltpu.SemaphoreType.DMA((ny, 2)),
        ],
        compiler_params=pltpu.CompilerParams(vmem_limit_bytes=48 * 1024 * 1024),
        cost_estimate=pl.CostEstimate(
            flops=20 * count * width * hidden,
            bytes_accessed=2 * (4 * count * width + 6 * width * hidden),
            transcendentals=2 * count * hidden,
        ),
    )(rows, others, *slices)


def shards(acts, cotangent, gain, router, ids, w_gate, w_up, w_down):
    ny, nx, nz, nc = (lax.axis_size(n) for n in ("y", "x", "z", "core"))
    y, x, core = (lax.axis_index(n) for n in ("y", "x", "core"))
    tokens, width = acts.shape
    top = ids.shape[1]
    experts = nz * nc
    cap = min(tokens, (17 * tokens * top + 16 * experts - 1) // (16 * experts))
    cap = -(-cap // 2)
    assert cap == MAIN + 1 and 2 * nz <= MAIN and ny % 2 == 0
    part = width // ny
    parity = x % 2
    swap = [(0, 1), (1, 0)]

    ahead, behind = [], []
    for j in range(ny):
        for i in range(nx):
            a = i % 2
            at = lambda yy, xx, cc: (yy * nx + xx % nx) * nc + cc
            ahead.append((at(j, i, 1 - a), at(j, i + 1, a)))
            behind.append((at(j, i, 1 - a), at(j, i - 1, a)))
            ahead.append((at(j, i, a), at(j ^ 1, i, a)))

    names = 2 * jnp.arange(nz, dtype=jnp.int32) + parity
    rows, sig, place = front_rows(acts, cotangent, gain, router, ids, nz, cap)
    mine = jnp.stack([w_gate[0].T, w_up[0].T, w_down[0]])
    left = lax.ppermute(mine, ("y", "x", "core"), behind)
    other = lax.ppermute(mine, ("y", "x", "core"), ahead)
    sig = sig.T
    total = jnp.sum(sig, axis=1, keepdims=True)
    weight = sig / total
    select = (ids[:, :, None] == jnp.arange(experts, dtype=jnp.int32)[None, None, :]).astype(f32)
    halves = [
        jnp.where((place >= n * cap) & (place < (n + 1) * cap), place - n * cap, -4096)
        for n in (0, 1)
    ]
    of_name = (ids[:, :, None] == names[None, None, :]).astype(f32)
    rows = lax.all_to_all(rows, "z", 0, 0, tiled=True)
    others = lax.ppermute(rows, "core", swap)

    pieces = part // LANE
    rank = -(-(pieces * cap + 4) // 8) * 8
    keep, give = expert_rows(rows, others, (mine, left, other), ny, rank)
    got = lax.ppermute(give, "core", swap)
    back = (keep.astype(f32) + got.astype(f32)).astype(bf16)

    back = lax.all_to_all(back.reshape(ny * nz, rank, LANE), ("y", "z"), 0, 0, tiled=True)
    flat = back.reshape(ny * nz * rank, LANE)
    by_y = [jnp.where(x // 2 % 2 == 1, halves[1 - n], halves[n]) for n in (0, 1)]
    parts = []
    for p in range(pieces):
        spread = []
        for slot in by_y:
            row = jnp.where(slot == MAIN, pieces * MAIN + p, slot + p * MAIN)
            spread.append(at_rows(jnp.where(slot >= 0, row, -1), rank).astype(bf16))
        spread = jnp.broadcast_to(jnp.stack(spread)[None], (ny // 2, 2, nz, rank, tokens))
        parts.append(
            lax.dot_general(
                spread.reshape(ny * nz * rank, tokens),
                flat,
                (((0,), (0,)), ((), ())),
                preferred_element_type=f32,
            )
        )
    score = jnp.sum(back[:, pieces * cap : pieces * cap + 4, :cap].astype(f32), axis=1)
    score = score.reshape(ny // 2, 2, nz, cap).sum(axis=0)
    slots = jnp.stack([at_rows(slot, cap) for slot in by_y]).astype(f32)
    score = jnp.sum(slots * score[:, :, :, None], axis=(0, 2))
    score = jnp.sum(of_name * score.T[:, None, :], axis=-1)
    sections = ny * nx
    share = tokens // sections
    high = score.astype(bf16)
    low = (score - high.astype(f32)).astype(bf16)
    tail = jnp.pad(jnp.concatenate([high, low], axis=1), ((0, 0), (0, LANE - 2 * top)))
    packet = [v.astype(bf16).reshape(sections, share, LANE) for v in parts] + [
        tail.reshape(sections, share, LANE)
    ]
    packet = jnp.stack(packet, axis=1).reshape(sections, (pieces + 1) * share, LANE)
    packet = lax.all_to_all(packet, ("y", "x"), 0, 0, tiled=True)
    packet = packet.reshape(ny, nx, pieces + 1, share, LANE).astype(f32).sum(axis=1)
    dh_share = packet[:, :pieces].transpose(2, 0, 1, 3).reshape(share, width)
    score_share = packet[0, pieces, :, :top] + packet[0, pieces, :, top : 2 * top]

    start = (y * nx + x) * share
    cut = lambda v: lax.dynamic_slice_in_dim(v, start, share, 0)
    sig, total, weight, select = cut(sig), cut(total), cut(weight), cut(select)
    wide = cut(acts).astype(f32)
    g = cut(cotangent).astype(f32)
    sent = weight.astype(bf16).astype(f32)
    score_share = jnp.where(sent > 0.0, score_share / jnp.where(sent > 0.0, sent, 1.0), 0.0)
    dsig = (score_share - jnp.sum(weight * score_share, axis=1, keepdims=True)) / total
    dpick = dsig * sig * (1.0 - sig)
    dlogits = jnp.sum(dpick[:, :, None] * select, axis=1)
    dh_total = dh_share + lax.dot_general(
        dlogits, router.astype(f32), (((1,), (1,)), ((), ())), precision=lax.Precision.HIGHEST
    )
    recip = lax.rsqrt(jnp.mean(wide * wide, axis=-1, keepdims=True) + eps)
    scaled = dh_total * gain
    pulled = recip * scaled - wide * (recip * recip * recip) * jnp.mean(
        wide * scaled, axis=-1, keepdims=True
    )
    return (g + pulled)[None]


def solution(mesh):
    pipe, expert = mesh.devices.shape
    grid = Mesh(
        mesh.devices.reshape(pipe // X, X, expert // CORES, CORES), ("y", "x", "z", "core")
    )
    exp, pipe = ("z", "core"), ("y", "x")
    in_specs = (
        P(exp, None),
        P(exp, None),
        P(),
        P(),
        P(exp, None),
        P(exp, None, pipe),
        P(exp, None, pipe),
        P(exp, pipe, None),
    )
    return jax.shard_map(
        shards, mesh=grid, in_specs=in_specs, out_specs=P(pipe, exp, None), check_vma=False
    )
```

```python
import functools
import jax
import jax.numpy as jnp
from jax import lax
from jax.experimental import pallas as pl
from jax.experimental.pallas import tpu as pltpu
from jax.sharding import Mesh, PartitionSpec as P

eps = 1e-05
X = 4
CORES = 2
LANE = 128
MAIN = 16
bf16 = jnp.bfloat16
f32 = jnp.float32


def at_rows(place, count):
    return place[:, None, :] == jnp.arange(count, dtype=jnp.int32)[None, :, None]


def front_kernel(cap, *refs):
    sources, weights, (out, sig_ref, place_ref, stacked) = refs[:5], refs[5:8], refs[8:12]
    copied, held, sem, stack_sem = refs[12:17], refs[17], refs[18], refs[19]
    copies = [
        pltpu.make_async_copy(source, ref, sem.at[i])
        for i, (source, ref) in enumerate(zip(sources, copied))
    ]
    loads = [
        pltpu.make_async_copy(weight, held.at[j], stack_sem.at[0, j])
        for j, weight in enumerate(weights)
    ]
    stores = [
        pltpu.make_async_copy(held.at[j], stacked.at[j], stack_sem.at[1, j])
        for j in range(len(weights))
    ]
    for copy in copies + loads:
        copy.start()
    for copy in copies:
        copy.wait()
    acts, cotangent, gain, router, ids = copied
    tokens, width = acts.shape
    nz, main, _ = out.shape
    top = ids.shape[0]
    fold = 2 * width // main
    x, y = lax.axis_index("x"), lax.axis_index("y")
    parity, odd = x % 2, (x // 2 + y) % 2
    wide = acts[...].astype(f32)
    recip = lax.rsqrt(jnp.mean(wide * wide, axis=1, keepdims=True) + eps)
    h = (wide * recip * gain[...]).astype(bf16)
    logits = lax.dot_general(
        router[...], h, (((1,), (1,)), ((), ())), preferred_element_type=f32
    )
    for load, store in zip(loads, stores):
        load.wait()
        store.start()
    named = lax.broadcasted_iota(jnp.int32, logits.shape, 0)
    sig = []
    for k in range(top):
        picked = jnp.where(named == ids[k : k + 1], logits, 0.0)
        sig.append(jax.nn.sigmoid(jnp.sum(picked, axis=0, keepdims=True)))
    sig_ref[...] = jnp.concatenate(sig, axis=0)
    total = sum(sig[1:], sig[0])
    names = 2 * lax.broadcasted_iota(jnp.int32, (nz, tokens), 0) + parity
    member = jnp.zeros((nz, tokens), f32)
    dense = jnp.zeros((nz, tokens), f32)
    for k in range(top):
        hit = names == ids[k : k + 1]
        member = jnp.where(hit, 1.0, member)
        dense = jnp.where(hit, sig[k] / total, dense)
    dense = dense.astype(bf16).astype(f32)
    before = lax.broadcasted_iota(jnp.int32, (tokens, tokens), 0)
    before = before < lax.broadcasted_iota(jnp.int32, (tokens, tokens), 1)
    place = jnp.dot(member.astype(bf16), before.astype(bf16), preferred_element_type=f32)
    place = jnp.where(member > 0.0, place.astype(jnp.int32), -4096)
    place_ref[...] = place
    place = place - odd * cap
    slot = lax.broadcasted_iota(jnp.int32, (main, tokens), 0)
    pick, scaled = [], []
    for z in range(nz):
        one = jnp.where(place[z : z + 1] == slot, 1.0, 0.0)
        pick.append(one)
        scaled.append(one * dense[z : z + 1])
    extra = jnp.where(place == main, 1.0, 0.0)
    sides = (
        (h, jnp.concatenate(pick, axis=0), extra),
        (cotangent[...], jnp.concatenate(scaled, axis=0), extra * dense),
    )
    folded = []
    for j, (values, mains, extras) in enumerate(sides):
        rows = jnp.dot(mains.astype(bf16), values, preferred_element_type=f32).astype(bf16)
        for z in range(nz):
            out[z, :, j * width : (j + 1) * width] = rows[z * main : (z + 1) * main]
        folded.append(jnp.dot(extras.astype(bf16), values, preferred_element_type=f32))
    for z in range(nz):
        lines = [v[z : z + 1, i * fold : (i + 1) * fold] for v in folded for i in range(main // 2)]
        out[z, :, 2 * width :] = jnp.concatenate(lines, axis=0).astype(bf16)
    for store in stores:
        store.wait()


def front_rows(acts, cotangent, gain, router, ids, weights, nz, cap):
    tokens, width = acts.shape
    vmem, hbm = (pl.BlockSpec(memory_space=m) for m in (pltpu.VMEM, pl.ANY))
    values = (acts, cotangent, gain.reshape(1, width), router.T, ids.T)
    return pl.pallas_call(
        functools.partial(front_kernel, cap),
        out_shape=(
            jax.ShapeDtypeStruct((nz, MAIN, 2 * width + 2 * width // MAIN), bf16),
            jax.ShapeDtypeStruct(ids.T.shape, f32),
            jax.ShapeDtypeStruct((nz, tokens), jnp.int32),
            jax.ShapeDtypeStruct((3, *weights[0].shape), bf16),
        ),
        in_specs=[hbm] * 8,
        out_specs=(vmem, vmem, vmem, hbm),
        scratch_shapes=[pltpu.VMEM(v.shape, v.dtype) for v in values]
        + [pltpu.VMEM((3, *weights[0].shape), bf16)]
        + [pltpu.SemaphoreType.DMA((5,)), pltpu.SemaphoreType.DMA((2, 3))],
        compiler_params=pltpu.CompilerParams(vmem_limit_bytes=60 * 1024 * 1024),
        cost_estimate=pl.CostEstimate(
            flops=4 * tokens * tokens * width,
            bytes_accessed=4 * tokens * width + 4 * nz * MAIN * width,
            transcendentals=tokens * 5,
        ),
    )(*values, *weights)


def expert_kernel(nz, rows_hbm, others_hbm, *refs):
    mine, left, other, keep_hbm, give_hbm = refs[:5]
    h_ref, g_ref, e_ref, w_ref, keep_ref, give_ref, row_sem, w_sem, out_sem = refs[5:]
    ny, rank, lane = keep_ref.shape[0], keep_ref.shape[2], keep_ref.shape[3]
    width = h_ref.shape[2]
    part, fold = width // ny, e_ref.shape[2]
    pieces = part // lane
    count = 2 * nz * MAIN
    contract = (((1,), (1,)), ((), ()))
    own = (lax.axis_index("core") == lax.axis_index("x") % 2).astype(jnp.int32)

    def fetch(u, j, source):
        return pltpu.make_async_copy(source.at[j], w_ref.at[u, j], w_sem.at[u, j])

    def start_first(j):
        @pl.when(own == 1)
        def _():
            fetch(0, j, mine).start()

        @pl.when(own == 0)
        def _():
            fetch(0, j, left).start()

    def begin(copies):
        for copy in copies:
            copy.start()

    def end(copies):
        for copy in copies:
            copy.wait()

    rows = []
    for j, (ref, first, size) in enumerate(
        ((h_ref, 0, width), (g_ref, width, width), (e_ref, 2 * width, fold))
    ):
        rows.append(
            [
                pltpu.make_async_copy(
                    source.at[:, :, pl.ds(first, size)],
                    ref.at[pl.ds(k * nz, nz)],
                    row_sem.at[j, k],
                )
                for k, source in enumerate((rows_hbm, others_hbm))
            ]
        )
    begin(rows[0] + rows[2])
    start_first(0)
    start_first(1)
    end(rows[0] + rows[2])
    begin(rows[1])
    start_first(2)
    half = MAIN // 2
    for i in range(half):
        band = pl.ds(i * fold, fold)
        h_ref[2 * nz, : 2 * nz, band] = e_ref[:, i, :]
    h = h_ref[...].reshape(count + MAIN, width)

    def times(u, j, value):
        return lax.dot_general(value, w_ref[u, j], contract, preferred_element_type=f32)

    a, b, dact = [None, None], [None, None], [None, None]
    fetch(0, 0, mine).wait()
    a[0] = times(0, 0, h)
    fetch(0, 1, mine).wait()
    fetch(1, 0, other).start()
    fetch(1, 1, other).start()
    b[0] = times(0, 1, h)
    end(rows[1])
    for i in range(half):
        band = pl.ds(i * fold, fold)
        g_ref[2 * nz, : 2 * nz, band] = e_ref[:, half + i, :]
    g = g_ref[...].reshape(count + MAIN, width)
    fetch(0, 2, mine).wait()
    fetch(1, 2, other).start()
    dact[0] = times(0, 2, g)
    fetch(1, 0, other).wait()
    a[1] = times(1, 0, h)
    fetch(1, 1, other).wait()
    b[1] = times(1, 1, h)
    fetch(1, 2, other).wait()
    dact[1] = times(1, 2, g)
    score = 0.0
    pulls = []
    for u in range(2):
        sg = jax.nn.sigmoid(a[u])
        sa = a[u] * sg
        act = (sa * b[u]).astype(bf16).astype(f32)
        score = score + jnp.sum(act * dact[u], axis=1, keepdims=True)
        pulls.append((dact[u] * b[u] * sg * (1.0 + a[u] * (1.0 - sg))).astype(bf16))
        pulls.append((dact[u] * sa).astype(bf16))
    lanes = lax.broadcasted_iota(jnp.int32, (MAIN, lane), 1)
    eye = lanes == lax.broadcasted_iota(jnp.int32, (MAIN, lane), 0)
    last = lax.broadcasted_iota(jnp.int32, (1, lane), 1) == MAIN
    gap = jnp.zeros((2, lane), f32)
    over = rank - pieces * (MAIN + 1) - 4
    rest = [jnp.zeros((over, lane), f32)] if over else []
    tails = []
    for n in range(2 * nz):
        line = jnp.where(eye, score[n * MAIN : (n + 1) * MAIN], 0.0)
        line = jnp.sum(line, axis=0, keepdims=True)
        line = line + jnp.where(last, score[count + n : count + n + 1], 0.0)
        high = line.astype(bf16).astype(f32)
        pair = [high, line - high]
        tails.append((pair + [gap] if n < nz else [gap] + pair) + rest)
    stores = []
    for i in range(ny):
        band = pl.ds(i * part, part)
        dh = 0.0
        for u in range(2):
            for j in range(2):
                dh = dh + jnp.dot(pulls[2 * u + j], w_ref[u, j, :, band], preferred_element_type=f32)
        for n in range(2 * nz):
            ref = keep_ref if n < nz else give_ref
            for p in range(pieces):
                cut = slice(p * lane, (p + 1) * lane)
                main = dh[n * MAIN : (n + 1) * MAIN, cut]
                ref[i, n % nz, p * MAIN : (p + 1) * MAIN] = main.astype(ref.dtype)
            end_rows = [
                dh[count + n : count + n + 1, p * lane : (p + 1) * lane] for p in range(pieces)
            ]
            ref[i, n % nz, pieces * MAIN :] = jnp.concatenate(end_rows + tails[n], axis=0).astype(
                ref.dtype
            )
        for j, (ref, hbm) in enumerate(((give_ref, give_hbm), (keep_ref, keep_hbm))):
            stores.append(pltpu.make_async_copy(ref.at[i], hbm.at[i], out_sem.at[i, j]))
            stores[-1].start()
    end(stores)


def expert_rows(rows, others, slices, ny, rank):
    nz = rows.shape[0]
    kinds, hidden, width = slices[0].shape
    hbm = pl.BlockSpec(memory_space=pl.ANY)
    count = (2 * nz + 1) * MAIN
    return pl.pallas_call(
        functools.partial(expert_kernel, nz),
        out_shape=(
            jax.ShapeDtypeStruct((ny, nz, rank, LANE), bf16),
            jax.ShapeDtypeStruct((ny, nz, rank, LANE), bf16),
        ),
        in_specs=[hbm] * 5,
        out_specs=(hbm, hbm),
        scratch_shapes=[
            pltpu.VMEM((2 * nz + 1, MAIN, width), bf16),
            pltpu.VMEM((2 * nz + 1, MAIN, width), bf16),
            pltpu.VMEM((2 * nz, MAIN, 2 * width // MAIN), bf16),
            pltpu.VMEM((2, kinds, hidden, width), bf16),
            pltpu.VMEM((ny, nz, rank, LANE), bf16),
            pltpu.VMEM((ny, nz, rank, LANE), bf16),
            pltpu.SemaphoreType.DMA((3, 2)),
            pltpu.SemaphoreType.DMA((2, 3)),
            pltpu.SemaphoreType.DMA((ny, 2)),
        ],
        compiler_params=pltpu.CompilerParams(vmem_limit_bytes=51 * 1024 * 1024),
        cost_estimate=pl.CostEstimate(
            flops=20 * count * width * hidden,
            bytes_accessed=2 * (4 * count * width + 6 * width * hidden),
            transcendentals=2 * count * hidden,
        ),
    )(rows, others, *slices)


def shards(acts, cotangent, gain, router, ids, w_gate, w_up, w_down):
    ny, nx, nz, nc = (lax.axis_size(n) for n in ("y", "x", "z", "core"))
    y, x, core = (lax.axis_index(n) for n in ("y", "x", "core"))
    tokens, width = acts.shape
    top = ids.shape[1]
    experts = nz * nc
    cap = min(tokens, (17 * tokens * top + 16 * experts - 1) // (16 * experts))
    cap = -(-cap // 2)
    assert cap == MAIN + 1 and 2 * nz <= MAIN and ny % 2 == 0
    part = width // ny
    parity = x % 2
    swap = [(0, 1), (1, 0)]

    ahead, behind = [], []
    for j in range(ny):
        for i in range(nx):
            a = i % 2
            at = lambda yy, xx, cc: (yy * nx + xx % nx) * nc + cc
            ahead.append((at(j, i, 1 - a), at(j, i + 1, a)))
            behind.append((at(j, i, 1 - a), at(j, i - 1, a)))
            ahead.append((at(j, i, a), at(j ^ 1, i, a)))

    names = 2 * jnp.arange(nz, dtype=jnp.int32) + parity
    weights = (w_gate[0].T, w_up[0].T, w_down[0])
    rows, sig, place, mine = front_rows(acts, cotangent, gain, router, ids, weights, nz, cap)
    left = lax.ppermute(mine, ("y", "x", "core"), behind)
    other = lax.ppermute(mine, ("y", "x", "core"), ahead)
    sig = sig.T
    total = jnp.sum(sig, axis=1, keepdims=True)
    weight = sig / total
    select = (ids[:, :, None] == jnp.arange(experts, dtype=jnp.int32)[None, None, :]).astype(f32)
    halves = [
        jnp.where((place >= n * cap) & (place < (n + 1) * cap), place - n * cap, -4096)
        for n in (0, 1)
    ]
    of_name = (ids[:, :, None] == names[None, None, :]).astype(f32)
    rows = lax.all_to_all(rows, "z", 0, 0, tiled=True)
    others = lax.ppermute(rows, "core", swap)

    pieces = part // LANE
    rank = -(-(pieces * cap + 4) // 8) * 8
    keep, give = expert_rows(rows, others, (mine, left, other), ny, rank)
    got = lax.ppermute(give, "core", swap)
    back = (keep.astype(f32) + got.astype(f32)).astype(bf16)

    back = lax.all_to_all(back.reshape(ny * nz, rank, LANE), ("y", "z"), 0, 0, tiled=True)
    flat = back.reshape(ny * nz * rank, LANE)
    by_y = [jnp.where(x // 2 % 2 == 1, halves[1 - n], halves[n]) for n in (0, 1)]
    parts = []
    for p in range(pieces):
        spread = []
        for slot in by_y:
            row = jnp.where(slot == MAIN, pieces * MAIN + p, slot + p * MAIN)
            spread.append(at_rows(jnp.where(slot >= 0, row, -1), rank).astype(bf16))
        spread = jnp.broadcast_to(jnp.stack(spread)[None], (ny // 2, 2, nz, rank, tokens))
        parts.append(
            lax.dot_general(
                spread.reshape(ny * nz * rank, tokens),
                flat,
                (((0,), (0,)), ((), ())),
                preferred_element_type=f32,
            )
        )
    score = jnp.sum(back[:, pieces * cap : pieces * cap + 4, :cap].astype(f32), axis=1)
    score = score.reshape(ny // 2, 2, nz, cap).sum(axis=0)
    slots = jnp.stack([at_rows(slot, cap) for slot in by_y]).astype(f32)
    score = jnp.sum(slots * score[:, :, :, None], axis=(0, 2))
    score = jnp.sum(of_name * score.T[:, None, :], axis=-1)
    sections = ny * nx
    share = tokens // sections
    high = score.astype(bf16)
    low = (score - high.astype(f32)).astype(bf16)
    tail = jnp.pad(jnp.concatenate([high, low], axis=1), ((0, 0), (0, LANE - 2 * top)))
    packet = [v.astype(bf16).reshape(sections, share, LANE) for v in parts] + [
        tail.reshape(sections, share, LANE)
    ]
    packet = jnp.stack(packet, axis=1).reshape(sections, (pieces + 1) * share, LANE)
    packet = lax.all_to_all(packet, ("y", "x"), 0, 0, tiled=True)
    packet = packet.reshape(ny, nx, pieces + 1, share, LANE).astype(f32).sum(axis=1)
    dh_share = packet[:, :pieces].transpose(2, 0, 1, 3).reshape(share, width)
    score_share = packet[0, pieces, :, :top] + packet[0, pieces, :, top : 2 * top]

    start = (y * nx + x) * share
    cut = lambda v: lax.dynamic_slice_in_dim(v, start, share, 0)
    sig, total, weight, select = cut(sig), cut(total), cut(weight), cut(select)
    wide = cut(acts).astype(f32)
    g = cut(cotangent).astype(f32)
    sent = weight.astype(bf16).astype(f32)
    score_share = jnp.where(sent > 0.0, score_share / jnp.where(sent > 0.0, sent, 1.0), 0.0)
    dsig = (score_share - jnp.sum(weight * score_share, axis=1, keepdims=True)) / total
    dpick = dsig * sig * (1.0 - sig)
    dlogits = jnp.sum(dpick[:, :, None] * select, axis=1)
    dh_total = dh_share + lax.dot_general(
        dlogits, router.astype(f32), (((1,), (1,)), ((), ())), precision=lax.Precision.HIGHEST
    )
    recip = lax.rsqrt(jnp.mean(wide * wide, axis=-1, keepdims=True) + eps)
    scaled = dh_total * gain
    pulled = recip * scaled - wide * (recip * recip * recip) * jnp.mean(
        wide * scaled, axis=-1, keepdims=True
    )
    return (g + pulled)[None]


def solution(mesh):
    pipe, expert = mesh.devices.shape
    grid = Mesh(
        mesh.devices.reshape(pipe // X, X, expert // CORES, CORES), ("y", "x", "z", "core")
    )
    exp, pipe = ("z", "core"), ("y", "x")
    in_specs = (
        P(exp, None),
        P(exp, None),
        P(),
        P(),
        P(exp, None),
        P(exp, None, pipe),
        P(exp, None, pipe),
        P(exp, pipe, None),
    )
    return jax.shard_map(
        shards, mesh=grid, in_specs=in_specs, out_specs=P(pipe, exp, None), check_vma=False
    )
```
